32 devices in a mesh: row: 16 (over z, y, x), col: 2 (over core).
Axes of the slice: x: 2, y: 2, z: 4, core: 2. Of those that a mesh axis runs over, the one named last changes fastest.
Arguments:
- tiles: float32 [16, 2, 64, 128, 128], P('row', 'col'), may hold values from -0.125 to 0.125
- tile_rows: int32 [16, 2, 64], P('row', 'col'), may hold values from 0 to 15, as said below
- tile_cols: int32 [16, 2, 64], P('row', 'col'), may hold values from 0 to 63, as said below
- exponents: int32 [16384], P('col'), may hold values from 0 to 3
- u_basis: float32 [64, 32768], P(None, 'row'), may hold values from -6 to 6
- v_basis: float32 [64, 16384], P(None, ('col', 'row')), may hold values from -6 to 6
- prior: float32 [64, 64], replicated, may hold values from -0.75 to 0.75
Outputs:
- u_next: float32 [64, 32768], P(None, ('row', 'col'))
- v_next: float32 [64, 16384], P(None, ('col', 'row'))
- v_factor: float32 [64, 64], replicated
- u_factor: float32 [64, 64], replicated
The draws below stay inside these ranges and needn't reach their ends.
Inputs may be any that keep to these rules, and one draw needn't show every extreme that they name: `tile_rows`: within each grid cell every tile row of 0 to 15 appears exactly 64 / 16 times. `tile_cols`: within each grid cell every tile column of 0 to 63 appears exactly 64 / 64 times.
All inputs are finite; a program needn't handle non-finite values.
Results may differ from the reference program's by a relative error of at most 0.00018.
Values sent between devices are 32-bit elements; how exact they have to be, the bound alone decides.
A program may use at most 64 MiB of HBM per device.

```python
import math
import jax
import jax.numpy as jnp
from jax import lax

S = 64
TILE = 128
RT = 16
CT = 64
NT = 64
GR = 16
GC = 2
M = 32768
N = 16384
N_ROW = 16


def covering(key, length):
    repeats = NT // length
    keys = jax.random.split(key, GR * GC * repeats)
    perms = jax.vmap(lambda k: jax.random.permutation(k, length))(keys)
    return perms.reshape(GR, GC, NT).astype(jnp.int32)


def draw_tile_rows(key, part):
    return covering(jax.random.fold_in(key, 11), RT)


def draw_tile_cols(key, part):
    return covering(jax.random.fold_in(key, 23), CT)


def place_ends(result, own_key, least, largest):
    dims = result.shape
    index_at = [jax.random.randint(jax.random.fold_in(own_key, axis), (), 0, dims[axis]) for axis in range(len(dims))]
    result = result.at[tuple(index_at)].set(least)
    longest = dims.index(max(dims))
    index_at[longest] = (index_at[longest] + 1) % dims[longest]
    return result.at[tuple(index_at)].set(largest)


def level_of(key, extent, cuts, low, top_value):
    def one(position, shards_of):
        heights = jax.random.uniform(jax.random.fold_in(jax.random.fold_in(key, 6), position), (shards_of,), jnp.float32, low / len(cuts), top_value / len(cuts))
        return jnp.repeat(jnp.exp(heights), extent[position] // shards_of).reshape((-1,) + (1,) * (len(extent) - position - 1))

    factor_of = one(*cuts[0])
    for cut in cuts[1:]:
        factor_of = factor_of * one(*cut)
    return factor_of


def gaussian(own_key, dims, deviation, most, cuts=(), dtype=jnp.bfloat16):
    loudness = level_of(own_key, dims, cuts, -0.22, 0.18) if cuts else 1.0
    drawn = jax.random.normal(own_key, dims, jnp.float32) * deviation * loudness
    return jnp.minimum(jnp.maximum(drawn, -most), most).astype(dtype)


def setup_inputs(seed: int = 0) -> dict:
    seeds = jax.random.split(jax.random.key(seed), 8)
    tiles = gaussian(seeds[0], (GR, GC, NT, TILE, TILE), (N_ROW * NT * TILE // CT) ** -0.5, 0.125, ((0, 16), (1, 2)), jnp.float32)
    tile_rows = draw_tile_rows(jax.random.fold_in(seeds[7], 71), 0)
    tile_cols = draw_tile_cols(jax.random.fold_in(seeds[7], 71), 0)
    exponents = place_ends(jax.random.randint(seeds[3], (N,), 0, 4), jax.random.fold_in(seeds[3], 1), 0, 3).astype(jnp.int32)
    u_basis = gaussian(seeds[4], (S, M), 1.0, 6.0, ((1, 16),), jnp.float32)
    v_basis = gaussian(seeds[5], (S, N), 1.0, 6.0, ((1, 32),), jnp.float32)
    prior = gaussian(seeds[6], (S, S), S ** -0.5, 0.75, (), jnp.float32)
    return dict(tiles=tiles, tile_rows=tile_rows, tile_cols=tile_cols, exponents=exponents, u_basis=u_basis, v_basis=v_basis, prior=prior)


HIGH = lax.Precision.HIGHEST

def lower_solve(factor, rhs):
    return lax.linalg.triangular_solve(factor, rhs, left_side=True, lower=True)

def reference(tiles, tile_rows, tile_cols, exponents, u_basis, v_basis, prior):
    grid_rows, grid_cols, count, tl, _ = tiles.shape
    width, total_rows = u_basis.shape
    total_cols = v_basis.shape[1]
    tile_cols_all = total_cols // tl
    rows_tiles = total_rows // (grid_rows * tl)
    cols_tiles = tile_cols_all // grid_cols
    col_scale = jnp.exp2(-exponents.astype(jnp.float32))
    lowtri = jnp.tril(prior)
    offsets = (jnp.arange(grid_cols) * cols_tiles).astype(jnp.int32)
    global_cols = (tile_cols + offsets[None, :, None]).astype(jnp.int32)
    u_blocks = u_basis.reshape(width, grid_rows, rows_tiles, tl).transpose(1, 0, 2, 3)

    def left_step(acc, inputs):
        tile_r, rows_r, gcol_r, ublock = inputs
        picked = jnp.take(ublock, rows_r.reshape(-1), axis=1)
        prod = jnp.einsum('sta,tab->tsb', picked, tile_r.reshape(-1, tl, tl), precision=HIGH)
        acc = acc + jax.ops.segment_sum(prod, gcol_r.reshape(-1), num_segments=tile_cols_all)
        return (acc, None)
    acc0 = jnp.zeros((tile_cols_all, width, tl), jnp.float32)
    acc, _ = lax.scan(left_step, acc0, (tiles, tile_rows, global_cols, u_blocks))
    left = acc.transpose(1, 0, 2).reshape(width, total_cols) * col_scale
    pt = left - jnp.dot(lowtri, v_basis, precision=HIGH)
    gram = jnp.dot(pt, pt.T, precision=HIGH)
    v_factor = jnp.linalg.cholesky(gram / total_cols)
    v_next = lower_solve(v_factor, pt)
    scaled = (v_next * col_scale).reshape(width, tile_cols_all, tl)

    def right_step(carry, inputs):
        tile_r, rows_r, gcol_r = inputs
        picked = jnp.take(scaled, gcol_r.reshape(-1), axis=1)
        prod = jnp.einsum('stb,tab->tsa', picked, tile_r.reshape(-1, tl, tl), precision=HIGH)
        return (carry, jax.ops.segment_sum(prod, rows_r.reshape(-1), num_segments=rows_tiles))
    _, pieces = lax.scan(right_step, jnp.zeros((), jnp.float32), (tiles, tile_rows, global_cols))
    right = pieces.transpose(2, 0, 1, 3).reshape(width, total_rows)
    factor = math.sqrt(total_rows / total_cols)
    qt = factor * right - jnp.dot(v_factor.T, u_basis, precision=HIGH)
    ugram = jnp.dot(qt, qt.T, precision=HIGH)
    u_factor = jnp.linalg.cholesky(ugram / total_rows)
    u_next = lower_solve(u_factor, qt)
    return (u_next, v_next, v_factor, u_factor)
```

```python
import functools
import math

import jax
import jax.numpy as jnp
from jax import lax
from jax.experimental import pallas as pl
from jax.experimental.pallas import tpu as pltpu
from jax.sharding import PartitionSpec as P

F32 = jnp.float32
BF16 = jnp.bfloat16
HIGH = lax.Precision.HIGHEST
TL = 128
QUADS = 4


def split(x):
    hi = x.astype(BF16)
    return hi, (x - hi.astype(F32)).astype(BF16)


def fold(x):
    w = x.shape[0] // 2
    y = x[:w] + x[w:]
    return y + pltpu.roll(y, w, 1)


def pack(x):
    w = x.shape[0]
    lane = lax.broadcasted_iota(jnp.int32, (w // 2, 2 * w), 1)
    return jnp.where(lane < w, x[: w // 2], x[w // 2 :])


def unpack(x):
    w = x.shape[1] // 2
    lane = lax.broadcasted_iota(jnp.int32, x.shape, 1)
    y = pltpu.roll(x, w, 1)
    return jnp.concatenate([jnp.where(lane < w, x, y), jnp.where(lane < w, y, x)], axis=0)


def factor_pair(gram2):
    w = gram2.shape[0]
    row = lax.broadcasted_iota(jnp.int32, (w, 2 * w), 0)
    lane = lax.broadcasted_iota(jnp.int32, (w, 2 * w), 1)
    m = jnp.where(lane < w, gram2, jnp.where(lane - w == row, 1.0, 0.0).astype(F32))
    below = lax.broadcasted_iota(jnp.int32, (w, 1), 0)
    for j in range(w - 1):
        pivot_row = m[j : j + 1, :]
        inv = 1.0 / m[j : j + 1, j : j + 1]
        times = jnp.where(below > j, m[:, j : j + 1], 0.0)
        m = m - times * (pivot_row * inv)
    diag = jnp.sum(jnp.where(lane == row, m, 0.0), axis=1, keepdims=True)
    m = m * (1.0 / jnp.sqrt(diag))
    return jnp.where((lane >= w) | (lane >= row), m, 0.0)


def transpose_left(pair):
    w = pair.shape[0]
    return jnp.concatenate([pair, pair], axis=0).T[:w, :w]


def kernel(
    nr, nc, total_rows, total_cols,
    idx, tiles, u, expo, v, prior,
    u_out, v_out, vf_out, uf_out,
    u2, part, got, gotz, own, pt, prods, terms, got_terms, gz, g1, g2c, g2q, g2z, qt,
    rs_send, rs_recv, z_send, z_recv, az_send, az_recv, ag_send, ag_recv,
    t_send, t_recv, g1_send, g1_recv, gc_send, gc_recv, gq_send, gq_recv, gg_send, gg_recv,
):
    nz = nr // QUADS
    width = u.shape[0]
    half = width // 2
    rt = terms.shape[0]
    rtc = rt // nc
    tp = part.shape[3]
    each = tiles.shape[0] // rt
    me = lax.axis_index("row")
    mc = lax.axis_index("col")
    z = me // QUADS
    gi = me % QUADS
    gx = gi + 1 - 2 * (gi % 2)
    gy = gi + 2 - 4 * (gi // 2)
    gd = (QUADS - 1) - gi
    base = z * QUADS
    to_x = {"row": base + gx}
    to_y = {"row": base + gy}
    to_d = {"row": base + gd}

    def to_z(zz):
        return {"row": zz * QUADS + gi}

    def to_c(cc):
        return {"col": cc}

    pending = []

    def remote(src, dst, ssem, rsem, dev):
        return pltpu.make_async_remote_copy(
            src_ref=src, dst_ref=dst, send_sem=ssem, recv_sem=rsem, device_id=dev,
            device_id_type=pl.DeviceIdType.MESH,
        )

    def send(*a):
        c = remote(*a)
        c.start()
        pending.append(c)

    barrier = pltpu.get_barrier_semaphore()
    peers = [to_x, to_y, to_d]
    peers += [to_z((z + k) % nz) for k in range(1, nz)]
    peers += [to_c((mc + k) % nc) for k in range(1, nc)]
    for p in peers:
        pl.semaphore_signal(barrier, inc=1, device_id=p, device_id_type=pl.DeviceIdType.MESH)

    for r in range(rt):
        hi, lo = split(u[:, r * TL : (r + 1) * TL])
        u2[r, 0:width] = hi
        u2[r, width : 2 * width] = lo

    def left_tile(j):
        th, tl_ = split(tiles[idx[0, j]])
        both = jnp.concatenate([th, tl_], axis=1)
        x = jnp.dot(u2[idx[1, j]], both, preferred_element_type=F32)
        y = x[:width] + x[width:]
        return y[:, :TL] + y[:, TL:]

    def compute(k):
        zz = (z + 1 + k) % nz
        for n, q in enumerate((gd, gx, gy, gi)):
            def body(t, _, q=q):
                y = left_tile((zz * QUADS + q) * tp + t)
                part[zz, q, 0, t] = y[:half]
                part[zz, q, 1, t] = y[half:]
                return 0
            lax.fori_loop(0, tp, body, 0, unroll=True)
            if n == 0 and k == 0:
                pl.semaphore_wait(barrier, len(peers))
            if n == 0:
                send(part.at[zz, q, 0], got.at[k, 0], rs_send.at[k, 0], rs_recv.at[k, 0], to_x)
                send(part.at[zz, q, 1], got.at[k, 1], rs_send.at[k, 1], rs_recv.at[k, 1], to_y)
            elif n == 1:
                send(part.at[zz, q, 0], got.at[k, 2], rs_send.at[k, 2], rs_recv.at[k, 2], to_x)
            elif n == 2:
                send(part.at[zz, q, 1], got.at[k, 3], rs_send.at[k, 3], rs_recv.at[k, 3], to_y)

    def rs_wait(k, n):
        remote(got.at[k, n], got.at[k, n], rs_send.at[k, n], rs_recv.at[k, n], to_x).wait_recv()

    def step2(k):
        zz = (z + 1 + k) % nz
        rs_wait(k, 0)
        part[zz, gy, 0] = part[zz, gy, 0] + got[k, 0]
        send(part.at[zz, gy, 0], got.at[k, 4], rs_send.at[k, 4], rs_recv.at[k, 4], to_y)
        rs_wait(k, 1)
        part[zz, gx, 1] = part[zz, gx, 1] + got[k, 1]
        send(part.at[zz, gx, 1], got.at[k, 5], rs_send.at[k, 5], rs_recv.at[k, 5], to_x)

    def step3(k):
        zz = (z + 1 + k) % nz
        for n in (2, 3, 4, 5):
            rs_wait(k, n)
        part[zz, gi, 0] = part[zz, gi, 0] + (got[k, 2] + got[k, 4])
        part[zz, gi, 1] = part[zz, gi, 1] + (got[k, 3] + got[k, 5])
        if k < nz - 1:
            send(part.at[zz, gi], gotz.at[z], z_send.at[k], z_recv.at[z], to_z(zz))

    for k in range(nz + 2):
        if k < nz:
            compute(k)
        if k == 0:
            tri = lax.broadcasted_iota(jnp.int32, prior.shape, 0) >= lax.broadcasted_iota(
                jnp.int32, prior.shape, 1
            )
            low = jnp.where(tri, prior[...], 0.0)
            own[...] = jnp.dot(low, v[...], precision=HIGH, preferred_element_type=F32)
        if 1 <= k < nz + 1:
            step2(k - 1)
        if 2 <= k:
            step3(k - 2)

    def scale_of(j):
        e = expo[j]
        return jnp.where(e % 2 == 1, 0.5, 1.0) * jnp.where(e >= 2, 0.25, 1.0)

    for k in range(1, nz):
        zs = (z + k) % nz
        remote(gotz.at[zs], gotz.at[zs], z_send.at[k - 1], z_recv.at[zs], to_z(zs)).wait_recv()
    for t in range(tp):
        sc = scale_of(me * tp + t)
        for h in range(2):
            x = part[z, gi, h, t]
            for k in range(1, nz):
                x = x + gotz[(z + k) % nz, h, t]
            pt[z, gi, h, t] = x * sc - own[h * half : (h + 1) * half, t * TL : (t + 1) * TL]

    for k in range(1, nz):
        zs = (z + k) % nz
        send(pt.at[z, gi], pt.at[z, gi], az_send.at[k - 1], az_recv.at[z], to_z(zs))

    def ag(src, k, n, dev):
        send(src, src, ag_send.at[k, n], ag_recv.at[k, n], dev)

    def ag_wait(dst, k, n):
        remote(dst, dst, ag_send.at[k, n], ag_recv.at[k, n], to_x).wait_recv()

    def right_tiles(zz, q):
        def body(t, acc):
            j = (zz * QUADS + q) * tp + t
            x = jnp.concatenate([pt[zz, q, 0, t], pt[zz, q, 1, t]], axis=0)
            hi, lo = split(x)
            xx = jnp.concatenate([hi, lo], axis=0)
            acc = acc + lax.dot_general(
                xx, xx, (((1,), (1,)), ((), ())), preferred_element_type=F32
            )
            th, tl_ = split(tiles[idx[0, j]])
            both = jnp.concatenate([th, tl_], axis=0)
            xs = (xx.astype(F32) * scale_of(j)).astype(BF16)
            y = lax.dot_general(xs, both, (((1,), (1,)), ((), ())), preferred_element_type=F32)
            y = y[:width] + y[width:]
            prods[j] = y[:, :TL] + y[:, TL:]
            return acc
        gz[zz * QUADS + q] = lax.fori_loop(
            0, tp, body, jnp.zeros((2 * width, 2 * width), F32), unroll=True
        )

    def arrive(k):
        zs = (z + nz - k) % nz
        if k:
            remote(pt.at[zs, gi], pt.at[zs, gi], az_send.at[0], az_recv.at[zs], to_z(zs)).wait_recv()
        ag(pt.at[zs, gi, 0], k, 0, to_y)
        ag(pt.at[zs, gi, 1], k, 1, to_x)
        ag(pt.at[zs, gi, 0], k, 2, to_x)
        ag(pt.at[zs, gi, 1], k, 3, to_y)
        right_tiles(zs, gi)

    def relay(k):
        zs = (z + nz - k) % nz
        ag_wait(pt.at[zs, gy, 0], k, 0)
        ag(pt.at[zs, gy, 0], k, 4, to_x)
        ag_wait(pt.at[zs, gx, 1], k, 1)
        ag(pt.at[zs, gx, 1], k, 5, to_y)

    def finish(k):
        zs = (z + nz - k) % nz
        ag_wait(pt.at[zs, gx, 0], k, 2)
        right_tiles(zs, gx)
        ag_wait(pt.at[zs, gy, 1], k, 3)
        right_tiles(zs, gy)
        ag_wait(pt.at[zs, gd, 0], k, 4)
        ag_wait(pt.at[zs, gd, 1], k, 5)
        right_tiles(zs, gd)

    for k in range(nz + 2):
        if k < nz:
            arrive(k)
        if 1 <= k < nz + 1:
            relay(k - 1)
        if 2 <= k:
            finish(k - 2)

    g = lax.fori_loop(
        1, nr, lambda i, a: a + gz[i], gz[0]
    )
    g1[mc] = pack(fold(g))
    for k in range(1, nc):
        cc = (mc + k) % nc
        send(g1.at[mc], g1.at[mc], g1_send.at[k - 1], g1_recv.at[mc], to_c(cc))

    def row_terms(r, _):
        x = prods[idx[2, r * each]]
        for i in range(1, each):
            x = x + prods[idx[2, r * each + i]]
        terms[r] = x
        return 0
    lax.fori_loop(0, rt, row_terms, 0)
    for k in range(1, nc):
        cc = (mc + k) % nc
        send(terms.at[pl.ds(cc * rtc, rtc)], got_terms.at[mc], t_send.at[k - 1], t_recv.at[mc], to_c(cc))

    for k in range(1, nc):
        cc = (mc + k) % nc
        remote(g1.at[cc], g1.at[cc], g1_send.at[k - 1], g1_recv.at[cc], to_c(cc)).wait_recv()
    gs = g1[0]
    for cc in range(1, nc):
        gs = gs + g1[cc]
    pair = factor_pair(unpack(gs * (1.0 / total_cols)))
    vf_out[...] = transpose_left(pair)
    for t in range(tp):
        x = jnp.concatenate(
            [jnp.zeros((width, TL), F32), pt[z, gi, 0, t], pt[z, gi, 1, t]], axis=0
        )
        v_out[:, t * TL : (t + 1) * TL] = jnp.dot(
            pair, x, precision=HIGH, preferred_element_type=F32
        )

    for k in range(1, nc):
        cc = (mc + k) % nc
        remote(got_terms.at[cc], got_terms.at[cc], t_send.at[k - 1], t_recv.at[cc], to_c(cc)).wait_recv()
    root = math.sqrt(total_rows / total_cols)

    acc = jnp.zeros((2 * width, 2 * width), F32)
    for i in range(rtc):
        r = mc * rtc + i
        x = terms[r]
        for k in range(1, nc):
            x = x + got_terms[(mc + k) % nc, i]
        uu = u[:, pl.ds(pl.multiple_of(r * TL, TL), TL)]
        q = jnp.dot(
            pair, jnp.concatenate([-uu, root * x], axis=0), precision=HIGH, preferred_element_type=F32
        )
        qt[i] = q
        xx = jnp.concatenate(split(q), axis=0)
        acc = acc + lax.dot_general(xx, xx, (((1,), (1,)), ((), ())), preferred_element_type=F32)

    def sum_over(buf, mine, n, x, ssem, rsem, to):
        buf[mine] = x
        for k in range(1, n):
            send(buf.at[mine], buf.at[mine], ssem.at[k - 1], rsem.at[mine], to((mine + k) % n))
        for k in range(1, n):
            o = (mine + k) % n
            remote(buf.at[o], buf.at[o], ssem.at[k - 1], rsem.at[o], to(o)).wait_recv()
        y = buf[0]
        for o in range(1, n):
            y = y + buf[o]
        return y

    x = sum_over(g2c, mc, nc, pack(fold(acc)), gc_send, gc_recv, to_c)
    x = sum_over(g2q, gi, QUADS, x, gq_send, gq_recv, lambda q: {"row": base + q})
    x = sum_over(g2z, z, nz, x, gg_send, gg_recv, to_z)
    pair2 = factor_pair(unpack(x * (1.0 / total_rows)))
    uf_out[...] = transpose_left(pair2)
    for i in range(rtc):
        y = jnp.concatenate([jnp.zeros((width, TL), F32), qt[i]], axis=0)
        u_out[:, i * TL : (i + 1) * TL] = jnp.dot(
            pair2, y, precision=HIGH, preferred_element_type=F32
        )
    for c in pending:
        c.wait_send()


def per_device(tiles, tile_rows, tile_cols, exponents, u_basis, v_basis, prior):
    nr, nc = lax.axis_size("row"), lax.axis_size("col")
    nz = nr // QUADS
    local = tiles[0, 0]
    rows, cols = tile_rows[0, 0], tile_cols[0, 0]
    count = local.shape[0]
    width, block_rows = u_basis.shape
    block_cols = exponents.shape[0]
    rt, ct = block_rows // TL, block_cols // TL
    tp = ct // nr
    rtc = rt // nc
    half = width // 2
    k = jnp.arange(count, dtype=jnp.int32)
    hit = cols[:, None] == k[None, :]
    key = rows * count + k
    rank = jnp.sum((key[None, :] < key[:, None]).astype(jnp.int32), axis=1)
    place = rank[:, None] == k[None, :]
    idx = jnp.stack([
        jnp.sum(jnp.where(hit, k[:, None], 0), axis=0),
        jnp.sum(jnp.where(hit, rows[:, None], 0), axis=0),
        jnp.sum(jnp.where(place, cols[:, None], 0), axis=0),
    ])
    expo = exponents.reshape(ct, 1, TL)
    dma = pltpu.SemaphoreType.DMA
    vm = pl.BlockSpec(memory_space=pltpu.VMEM)

    def sems(*shape):
        return [dma(shape), dma(shape)]

    return pl.pallas_call(
        functools.partial(kernel, nr, nc, block_rows * nr, block_cols * nc),
        out_shape=(
            jax.ShapeDtypeStruct((width, block_rows // nc), F32),
            jax.ShapeDtypeStruct((width, block_cols // nr), F32),
            jax.ShapeDtypeStruct((width, width), F32),
            jax.ShapeDtypeStruct((width, width), F32),
        ),
        in_specs=[pl.BlockSpec(memory_space=pltpu.SMEM)] + [vm] * 5,
        out_specs=(vm,) * 4,
        scratch_shapes=[
            pltpu.VMEM((rt, 2 * width, TL), BF16),
            pltpu.VMEM((nz, QUADS, 2, tp, half, TL), F32),
            pltpu.VMEM((nz, 6, tp, half, TL), F32),
            pltpu.VMEM((nz, 2, tp, half, TL), F32),
            pltpu.VMEM((width, tp * TL), F32),
            pltpu.VMEM((nz, QUADS, 2, tp, half, TL), F32),
            pltpu.VMEM((ct, width, TL), F32),
            pltpu.VMEM((rt, width, TL), F32),
            pltpu.VMEM((nc, rtc, width, TL), F32),
            pltpu.VMEM((nr, 2 * width, 2 * width), F32),
            pltpu.VMEM((nc, half, 2 * width), F32),
            pltpu.VMEM((nc, half, 2 * width), F32),
            pltpu.VMEM((QUADS, half, 2 * width), F32),
            pltpu.VMEM((nz, half, 2 * width), F32),
            pltpu.VMEM((rtc, width, TL), F32),
            *sems(nz, 6),
            dma((nz,)), dma((nz,)),
            dma((nz,)), dma((nz,)),
            *sems(nz, 6),
            dma((nc,)), dma((nc,)),
            dma((nc,)), dma((nc,)),
            dma((nc,)), dma((nc,)),
            dma((QUADS,)), dma((QUADS,)),
            dma((nz,)), dma((nz,)),
        ],
        compiler_params=pltpu.CompilerParams(
            collective_id=0, has_side_effects=True, vmem_limit_bytes=48 * 1024 * 1024
        ),
    )(idx, local, u_basis, expo, v_basis, prior)


def solution(mesh):
    placed = (
        P("row", "col", None, None, None),
        P("row", "col", None),
        P("row", "col", None),
        P("col"),
        P(None, "row"),
        P(None, ("col", "row")),
        P(),
    )
    return jax.shard_map(
        per_device,
        mesh=mesh,
        in_specs=placed,
        out_specs=(P(None, ("row", "col")), P(None, ("col", "row")), P(), P()),
        check_vma=False,
    )
```

```python
import functools
import math

import jax
import jax.numpy as jnp
from jax import lax
from jax.experimental import pallas as pl
from jax.experimental.pallas import tpu as pltpu
from jax.sharding import PartitionSpec as P

F32 = jnp.float32
BF16 = jnp.bfloat16
HIGH = lax.Precision.HIGHEST
TL = 128
QUADS = 4


def split(x):
    hi = x.astype(BF16)
    return hi, (x - hi.astype(F32)).astype(BF16)


def fold(x):
    w = x.shape[0] // 2
    y = x[:w] + x[w:]
    return y + pltpu.roll(y, w, 1)


def pack(x):
    w = x.shape[0]
    lane = lax.broadcasted_iota(jnp.int32, (w // 2, 2 * w), 1)
    return jnp.where(lane < w, x[: w // 2], x[w // 2 :])


def unpack(x):
    w = x.shape[1] // 2
    lane = lax.broadcasted_iota(jnp.int32, x.shape, 1)
    y = pltpu.roll(x, w, 1)
    return jnp.concatenate([jnp.where(lane < w, x, y), jnp.where(lane < w, y, x)], axis=0)


def factor_pair(gram2, block=4):
    w = gram2.shape[0]
    row = lax.broadcasted_iota(jnp.int32, (w, 2 * w), 0)
    lane = lax.broadcasted_iota(jnp.int32, (w, 2 * w), 1)
    m = jnp.where(lane < w, gram2, jnp.where(lane - w == row, 1.0, 0.0).astype(F32))
    done, top = [], 0
    for j in range(0, w, block):
        o = j - top
        below = row[top:]
        cols = [jnp.broadcast_to(m[:, j + i : j + i + 1], m.shape) for i in range(block)]
        rows = [m[o + i : o + i + 1] for i in range(block)]
        a = {(i, l): cols[l][o + i : o + i + 1] for i in range(block) for l in range(i, block)}
        for i in range(block):
            inv = 1.0 / a[i, i]
            m = m - jnp.where(below > j + i, cols[i], 0.0) * (rows[i] * inv)
            for l in range(i + 1, block):
                s = a[i, l] * inv
                rows[l] = rows[l] - s * rows[i]
                cols[l] = cols[l] - s * cols[i]
                for q in range(l, block):
                    a[l, q] = a[l, q] - s * a[i, q]
        if (j + block) % 8 == 0:
            done.append(m[:8])
            m = m[8:]
            top += 8
    m = jnp.concatenate(done, axis=0)
    diag = jnp.sum(jnp.where(lane == row, m, 0.0), axis=1, keepdims=True)
    m = m * (1.0 / jnp.sqrt(diag))
    return jnp.where((lane >= w) | (lane >= row), m, 0.0)


def transpose_left(pair):
    w = pair.shape[0]
    return jnp.concatenate([pair, pair], axis=0).T[:w, :w]


def tile_lists(rows_in, cols_in, lists, row_count, col_count):
    n = rows_in.shape[1]
    rows = jnp.broadcast_to(rows_in[...], (n, n))
    cols = jnp.broadcast_to(cols_in[...], (n, n))
    down = lax.broadcasted_iota(jnp.int32, (n, n), 0)
    across = lax.broadcasted_iota(jnp.int32, (n, n), 1)
    key = rows * n + across
    key_down = jnp.sum(jnp.where(down == across, key, 0), axis=1, keepdims=True)
    rank = jnp.sum(jnp.where(key_down < key, 1, 0), axis=0, keepdims=True)
    hit = cols == down
    tile = jnp.max(jnp.where(hit, across, 0), axis=1, keepdims=True)
    tile_row = jnp.clip(jnp.max(jnp.where(hit, rows, 0), axis=1, keepdims=True), 0, row_count - 1)
    ordered = jnp.clip(
        jnp.max(jnp.where(rank == down, cols, 0), axis=1, keepdims=True), 0, col_count - 1
    )
    lane = lax.broadcasted_iota(jnp.int32, lists.shape, 1)
    lists[...] = jnp.where(lane == 0, tile, jnp.where(lane == 1, tile_row, ordered))


def kernel(
    nr, nc, total_rows, total_cols,
    rows_hbm, cols_hbm, tiles_hbm, u_hbm, expo_hbm, v_hbm, prior_hbm,
    u_out, v_out, vf_out, uf_out,
    rows_in, cols_in, tiles, u, expo, v, prior, lists, idx, in_sem,
    u2, part, got, gotz, own, pt, prods, terms, got_terms, gz, g1, g2c, g2q, g2z, qt,
    rs_send, rs_recv, z_send, z_recv, az_send, az_recv, ag_send, ag_recv,
    t_send, t_recv, g1_send, g1_recv, gc_send, gc_recv, gq_send, gq_recv, gg_send, gg_recv,
):
    nz = nr // QUADS
    width = u.shape[0]
    half = width // 2
    rt = terms.shape[0]
    rtc = rt // nc
    tp = part.shape[3]
    each = tiles.shape[0] // rt
    me = lax.axis_index("row")
    mc = lax.axis_index("col")
    z = me // QUADS
    gi = me % QUADS
    gx = gi + 1 - 2 * (gi % 2)
    gy = gi + 2 - 4 * (gi // 2)
    gd = (QUADS - 1) - gi
    base = z * QUADS
    to_x = {"row": base + gx}
    to_y = {"row": base + gy}
    to_d = {"row": base + gd}

    def to_z(zz):
        return {"row": zz * QUADS + gi}

    def to_c(cc):
        return {"col": cc}

    pending = []

    def remote(src, dst, ssem, rsem, dev):
        return pltpu.make_async_remote_copy(
            src_ref=src, dst_ref=dst, send_sem=ssem, recv_sem=rsem, device_id=dev,
            device_id_type=pl.DeviceIdType.MESH,
        )

    def send(*a):
        c = remote(*a)
        c.start()
        pending.append(c)

    fetch = [
        pltpu.make_async_copy(src, dst, in_sem.at[i])
        for i, (src, dst) in enumerate((
            (rows_hbm, rows_in), (cols_hbm, cols_in), (u_hbm, u), (tiles_hbm, tiles),
            (expo_hbm, expo), (v_hbm, v), (prior_hbm, prior),
        ))
    ]
    for c in fetch:
        c.start()
    barrier = pltpu.get_barrier_semaphore()
    peers = [to_x, to_y, to_d]
    peers += [to_z((z + k) % nz) for k in range(1, nz)]
    peers += [to_c((mc + k) % nc) for k in range(1, nc)]
    for p in peers:
        pl.semaphore_signal(barrier, inc=1, device_id=p, device_id_type=pl.DeviceIdType.MESH)

    for c in fetch[:2]:
        c.wait()
    tile_lists(rows_in, cols_in, lists, rt, expo.shape[0])
    to_scalars = pltpu.make_async_copy(lists, idx, in_sem.at[len(fetch)])
    to_scalars.start()
    fetch[2].wait()
    for r in range(rt):
        hi, lo = split(u[:, r * TL : (r + 1) * TL])
        u2[r, 0:width] = hi
        u2[r, width : 2 * width] = lo

    to_scalars.wait()
    for c in fetch[3:]:
        c.wait()

    def left_tile(j):
        th, tl_ = split(tiles[idx[j, 0]])
        both = jnp.concatenate([th, tl_], axis=1)
        x = jnp.dot(u2[idx[j, 1]], both, preferred_element_type=F32)
        y = x[:width] + x[width:]
        return y[:, :TL] + y[:, TL:]

    def compute(k):
        zz = (z + 1 + k) % nz
        for n, q in enumerate((gd, gx, gy, gi)):
            def body(t, _, q=q):
                y = left_tile((zz * QUADS + q) * tp + t)
                part[zz, q, 0, t] = y[:half]
                part[zz, q, 1, t] = y[half:]
                return 0
            lax.fori_loop(0, tp, body, 0, unroll=True)
            if n == 0 and k == 0:
                pl.semaphore_wait(barrier, len(peers))
            if n == 0:
                send(part.at[zz, q, 0], got.at[k, 0], rs_send.at[k, 0], rs_recv.at[k, 0], to_x)
                send(part.at[zz, q, 1], got.at[k, 1], rs_send.at[k, 1], rs_recv.at[k, 1], to_y)
            elif n == 1:
                send(part.at[zz, q, 0], got.at[k, 2], rs_send.at[k, 2], rs_recv.at[k, 2], to_x)
            elif n == 2:
                send(part.at[zz, q, 1], got.at[k, 3], rs_send.at[k, 3], rs_recv.at[k, 3], to_y)

    def rs_wait(k, n):
        remote(got.at[k, n], got.at[k, n], rs_send.at[k, n], rs_recv.at[k, n], to_x).wait_recv()

    def step2(k):
        zz = (z + 1 + k) % nz
        rs_wait(k, 0)
        part[zz, gy, 0] = part[zz, gy, 0] + got[k, 0]
        send(part.at[zz, gy, 0], got.at[k, 4], rs_send.at[k, 4], rs_recv.at[k, 4], to_y)
        rs_wait(k, 1)
        part[zz, gx, 1] = part[zz, gx, 1] + got[k, 1]
        send(part.at[zz, gx, 1], got.at[k, 5], rs_send.at[k, 5], rs_recv.at[k, 5], to_x)

    def step3(k):
        zz = (z + 1 + k) % nz
        for n in (2, 3, 4, 5):
            rs_wait(k, n)
        part[zz, gi, 0] = part[zz, gi, 0] + (got[k, 2] + got[k, 4])
        part[zz, gi, 1] = part[zz, gi, 1] + (got[k, 3] + got[k, 5])
        if k < nz - 1:
            send(part.at[zz, gi], gotz.at[z], z_send.at[k], z_recv.at[z], to_z(zz))

    for k in range(nz + 2):
        if k < nz:
            compute(k)
        if k == 0:
            tri = lax.broadcasted_iota(jnp.int32, prior.shape, 0) >= lax.broadcasted_iota(
                jnp.int32, prior.shape, 1
            )
            low = jnp.where(tri, prior[...], 0.0)
            own[...] = jnp.dot(low, v[...], precision=HIGH, preferred_element_type=F32)
        if 1 <= k < nz + 1:
            step2(k - 1)
        if 2 <= k:
            step3(k - 2)

    def scale_of(j):
        e = expo[j]
        return jnp.where(e % 2 == 1, 0.5, 1.0) * jnp.where(e >= 2, 0.25, 1.0)

    for k in range(1, nz):
        zs = (z + k) % nz
        remote(gotz.at[zs], gotz.at[zs], z_send.at[k - 1], z_recv.at[zs], to_z(zs)).wait_recv()
    for t in range(tp):
        sc = scale_of(me * tp + t)
        for h in range(2):
            x = part[z, gi, h, t]
            for k in range(1, nz):
                x = x + gotz[(z + k) % nz, h, t]
            pt[z, gi, h, t] = x * sc - own[h * half : (h + 1) * half, t * TL : (t + 1) * TL]

    for k in range(1, nz):
        zs = (z + k) % nz
        send(pt.at[z, gi], pt.at[z, gi], az_send.at[k - 1], az_recv.at[z], to_z(zs))

    def ag(src, k, n, dev):
        send(src, src, ag_send.at[k, n], ag_recv.at[k, n], dev)

    def ag_wait(dst, k, n):
        remote(dst, dst, ag_send.at[k, n], ag_recv.at[k, n], to_x).wait_recv()

    def right_tiles(zz, q):
        def body(t, acc):
            j = (zz * QUADS + q) * tp + t
            x = jnp.concatenate([pt[zz, q, 0, t], pt[zz, q, 1, t]], axis=0)
            hi, lo = split(x)
            xx = jnp.concatenate([hi, lo], axis=0)
            acc = acc + lax.dot_general(
                xx, xx, (((1,), (1,)), ((), ())), preferred_element_type=F32
            )
            th, tl_ = split(tiles[idx[j, 0]])
            both = jnp.concatenate([th, tl_], axis=0)
            xs = (xx.astype(F32) * scale_of(j)).astype(BF16)
            y = lax.dot_general(xs, both, (((1,), (1,)), ((), ())), preferred_element_type=F32)
            y = y[:width] + y[width:]
            prods[j] = y[:, :TL] + y[:, TL:]
            return acc
        gz[zz * QUADS + q] = lax.fori_loop(
            0, tp, body, jnp.zeros((2 * width, 2 * width), F32), unroll=True
        )

    def arrive(k):
        zs = (z + nz - k) % nz
        if k:
            remote(pt.at[zs, gi], pt.at[zs, gi], az_send.at[0], az_recv.at[zs], to_z(zs)).wait_recv()
        ag(pt.at[zs, gi, 0], k, 0, to_y)
        ag(pt.at[zs, gi, 1], k, 1, to_x)
        ag(pt.at[zs, gi, 0], k, 2, to_x)
        ag(pt.at[zs, gi, 1], k, 3, to_y)
        right_tiles(zs, gi)

    def relay(k):
        zs = (z + nz - k) % nz
        ag_wait(pt.at[zs, gy, 0], k, 0)
        ag(pt.at[zs, gy, 0], k, 4, to_x)
        ag_wait(pt.at[zs, gx, 1], k, 1)
        ag(pt.at[zs, gx, 1], k, 5, to_y)

    def finish(k):
        zs = (z + nz - k) % nz
        ag_wait(pt.at[zs, gx, 0], k, 2)
        right_tiles(zs, gx)
        ag_wait(pt.at[zs, gy, 1], k, 3)
        right_tiles(zs, gy)
        ag_wait(pt.at[zs, gd, 0], k, 4)
        ag_wait(pt.at[zs, gd, 1], k, 5)
        right_tiles(zs, gd)

    for k in range(nz + 2):
        if k < nz:
            arrive(k)
        if 1 <= k < nz + 1:
            relay(k - 1)
        if 2 <= k:
            finish(k - 2)

    g = lax.fori_loop(
        1, nr, lambda i, a: a + gz[i], gz[0]
    )
    g1[mc] = pack(fold(g))
    for k in range(1, nc):
        cc = (mc + k) % nc
        send(g1.at[mc], g1.at[mc], g1_send.at[k - 1], g1_recv.at[mc], to_c(cc))

    def row_terms(r, _):
        x = prods[idx[r * each, 2]]
        for i in range(1, each):
            x = x + prods[idx[r * each + i, 2]]
        terms[r] = x
        return 0
    lax.fori_loop(0, rt, row_terms, 0)
    for k in range(1, nc):
        cc = (mc + k) % nc
        send(terms.at[pl.ds(cc * rtc, rtc)], got_terms.at[mc], t_send.at[k - 1], t_recv.at[mc], to_c(cc))

    for k in range(1, nc):
        cc = (mc + k) % nc
        remote(g1.at[cc], g1.at[cc], g1_send.at[k - 1], g1_recv.at[cc], to_c(cc)).wait_recv()
    gs = g1[0]
    for cc in range(1, nc):
        gs = gs + g1[cc]
    pair = factor_pair(unpack(gs * (1.0 / total_cols)))
    vf_out[...] = transpose_left(pair)
    for t in range(tp):
        x = jnp.concatenate(
            [jnp.zeros((width, TL), F32), pt[z, gi, 0, t], pt[z, gi, 1, t]], axis=0
        )
        v_out[:, t * TL : (t + 1) * TL] = jnp.dot(
            pair, x, precision=HIGH, preferred_element_type=F32
        )

    for k in range(1, nc):
        cc = (mc + k) % nc
        remote(got_terms.at[cc], got_terms.at[cc], t_send.at[k - 1], t_recv.at[cc], to_c(cc)).wait_recv()
    root = math.sqrt(total_rows / total_cols)

    acc = jnp.zeros((2 * width, 2 * width), F32)
    for i in range(rtc):
        r = mc * rtc + i
        x = terms[r]
        for k in range(1, nc):
            x = x + got_terms[(mc + k) % nc, i]
        uu = u[:, pl.ds(pl.multiple_of(r * TL, TL), TL)]
        q = jnp.dot(
            pair, jnp.concatenate([-uu, root * x], axis=0), precision=HIGH, preferred_element_type=F32
        )
        qt[i] = q
        xx = jnp.concatenate(split(q), axis=0)
        acc = acc + lax.dot_general(xx, xx, (((1,), (1,)), ((), ())), preferred_element_type=F32)

    def sum_over(buf, mine, n, x, ssem, rsem, to):
        buf[mine] = x
        for k in range(1, n):
            send(buf.at[mine], buf.at[mine], ssem.at[k - 1], rsem.at[mine], to((mine + k) % n))
        for k in range(1, n):
            o = (mine + k) % n
            remote(buf.at[o], buf.at[o], ssem.at[k - 1], rsem.at[o], to(o)).wait_recv()
        y = buf[0]
        for o in range(1, n):
            y = y + buf[o]
        return y

    x = sum_over(g2c, mc, nc, pack(fold(acc)), gc_send, gc_recv, to_c)
    x = sum_over(g2q, gi, QUADS, x, gq_send, gq_recv, lambda q: {"row": base + q})
    x = sum_over(g2z, z, nz, x, gg_send, gg_recv, to_z)
    pair2 = factor_pair(unpack(x * (1.0 / total_rows)))
    uf_out[...] = transpose_left(pair2)
    for i in range(rtc):
        y = jnp.concatenate([jnp.zeros((width, TL), F32), qt[i]], axis=0)
        u_out[:, i * TL : (i + 1) * TL] = jnp.dot(
            pair2, y, precision=HIGH, preferred_element_type=F32
        )
    for c in pending:
        c.wait_send()


def per_device(tiles, tile_rows, tile_cols, exponents, u_basis, v_basis, prior):
    nr, nc = lax.axis_size("row"), lax.axis_size("col")
    nz = nr // QUADS
    local = tiles[0, 0]
    rows, cols = tile_rows[0], tile_cols[0]
    count = local.shape[0]
    width, block_rows = u_basis.shape
    block_cols = exponents.shape[0]
    rt, ct = block_rows // TL, block_cols // TL
    tp = ct // nr
    rtc = rt // nc
    half = width // 2
    expo = exponents.reshape(ct, 1, TL)
    dma = pltpu.SemaphoreType.DMA
    vm = pl.BlockSpec(memory_space=pltpu.VMEM)

    def sems(*shape):
        return [dma(shape), dma(shape)]

    return pl.pallas_call(
        functools.partial(kernel, nr, nc, block_rows * nr, block_cols * nc),
        out_shape=(
            jax.ShapeDtypeStruct((width, block_rows // nc), F32),
            jax.ShapeDtypeStruct((width, block_cols // nr), F32),
            jax.ShapeDtypeStruct((width, width), F32),
            jax.ShapeDtypeStruct((width, width), F32),
        ),
        in_specs=[pl.BlockSpec(memory_space=pl.ANY)] * 7,
        out_specs=(vm,) * 4,
        scratch_shapes=[
            pltpu.VMEM((1, count), jnp.int32),
            pltpu.VMEM((1, count), jnp.int32),
            pltpu.VMEM((count, TL, TL), F32),
            pltpu.VMEM((width, block_rows), F32),
            pltpu.VMEM((ct, 1, TL), jnp.int32),
            pltpu.VMEM((width, tp * TL), F32),
            pltpu.VMEM((width, width), F32),
            pltpu.VMEM((count, TL), jnp.int32),
            pltpu.SMEM((count, TL), jnp.int32),
            dma((8,)),
            pltpu.VMEM((rt, 2 * width, TL), BF16),
            pltpu.VMEM((nz, QUADS, 2, tp, half, TL), F32),
            pltpu.VMEM((nz, 6, tp, half, TL), F32),
            pltpu.VMEM((nz, 2, tp, half, TL), F32),
            pltpu.VMEM((width, tp * TL), F32),
            pltpu.VMEM((nz, QUADS, 2, tp, half, TL), F32),
            pltpu.VMEM((ct, width, TL), F32),
            pltpu.VMEM((rt, width, TL), F32),
            pltpu.VMEM((nc, rtc, width, TL), F32),
            pltpu.VMEM((nr, 2 * width, 2 * width), F32),
            pltpu.VMEM((nc, half, 2 * width), F32),
            pltpu.VMEM((nc, half, 2 * width), F32),
            pltpu.VMEM((QUADS, half, 2 * width), F32),
            pltpu.VMEM((nz, half, 2 * width), F32),
            pltpu.VMEM((rtc, width, TL), F32),
            *sems(nz, 6),
            dma((nz,)), dma((nz,)),
            dma((nz,)), dma((nz,)),
            *sems(nz, 6),
            dma((nc,)), dma((nc,)),
            dma((nc,)), dma((nc,)),
            dma((nc,)), dma((nc,)),
            dma((QUADS,)), dma((QUADS,)),
            dma((nz,)), dma((nz,)),
        ],
        compiler_params=pltpu.CompilerParams(
            collective_id=0, has_side_effects=True, vmem_limit_bytes=56 * 1024 * 1024
        ),
    )(rows, cols, local, u_basis, expo, v_basis, prior)


def solution(mesh):
    placed = (
        P("row", "col", None, None, None),
        P("row", "col", None),
        P("row", "col", None),
        P("col"),
        P(None, "row"),
        P(None, ("col", "row")),
        P(),
    )
    return jax.shard_map(
        per_device,
        mesh=mesh,
        in_specs=placed,
        out_specs=(P(None, ("row", "col")), P(None, ("col", "row")), P(), P()),
        check_vma=False,
    )
```

```python
import functools
import math

import jax
import jax.numpy as jnp
from jax import lax
from jax.experimental import pallas as pl
from jax.experimental.pallas import tpu as pltpu
from jax.sharding import PartitionSpec as P

F32 = jnp.float32
BF16 = jnp.bfloat16
HIGH = lax.Precision.HIGHEST
TL = 128
QUADS = 4


def split(x):
    hi = x.astype(BF16)
    return hi, (x - hi.astype(F32)).astype(BF16)


def fold(x):
    w = x.shape[0] // 2
    y = x[:w] + x[w:]
    return y + pltpu.roll(y, w, 1)


def pack(x):
    w = x.shape[0]
    lane = lax.broadcasted_iota(jnp.int32, (w // 2, 2 * w), 1)
    return jnp.where(lane < w, x[: w // 2], x[w // 2 :])


def unpack(x):
    w = x.shape[1] // 2
    lane = lax.broadcasted_iota(jnp.int32, x.shape, 1)
    y = pltpu.roll(x, w, 1)
    return jnp.concatenate([jnp.where(lane < w, x, y), jnp.where(lane < w, y, x)], axis=0)


def factor_pair(gram2, block=4):
    w = gram2.shape[0]
    row = lax.broadcasted_iota(jnp.int32, (w, 2 * w), 0)
    lane = lax.broadcasted_iota(jnp.int32, (w, 2 * w), 1)
    m = jnp.where(lane < w, gram2, jnp.where(lane - w == row, 1.0, 0.0).astype(F32))
    done, top = [], 0
    for j in range(0, w, block):
        o = j - top
        below = row[top:]
        cols = [jnp.broadcast_to(m[:, j + i : j + i + 1], m.shape) for i in range(block)]
        rows = [m[o + i : o + i + 1] for i in range(block)]
        a = {(i, l): cols[l][o + i : o + i + 1] for i in range(block) for l in range(i, block)}
        for i in range(block):
            inv = 1.0 / a[i, i]
            m = m - jnp.where(below > j + i, cols[i], 0.0) * (rows[i] * inv)
            for l in range(i + 1, block):
                s = a[i, l] * inv
                rows[l] = rows[l] - s * rows[i]
                cols[l] = cols[l] - s * cols[i]
                for q in range(l, block):
                    a[l, q] = a[l, q] - s * a[i, q]
        if (j + block) % 8 == 0:
            done.append(m[:8])
            m = m[8:]
            top += 8
    m = jnp.concatenate(done, axis=0)
    diag = jnp.sum(jnp.where(lane == row, m, 0.0), axis=1, keepdims=True)
    m = m * (1.0 / jnp.sqrt(diag))
    return jnp.where((lane >= w) | (lane >= row), m, 0.0)


def transpose_left(pair):
    w = pair.shape[0]
    return jnp.concatenate([pair, pair], axis=0).T[:w, :w]


def tile_lists(rows_in, cols_in, lists, row_count, col_count):
    n = rows_in.shape[1]
    rows = jnp.broadcast_to(rows_in[...], (n, n))
    cols = jnp.broadcast_to(cols_in[...], (n, n))
    down = lax.broadcasted_iota(jnp.int32, (n, n), 0)
    across = lax.broadcasted_iota(jnp.int32, (n, n), 1)
    key = rows * n + across
    key_down = jnp.sum(jnp.where(down == across, key, 0), axis=1, keepdims=True)
    rank = jnp.sum(jnp.where(key_down < key, 1, 0), axis=0, keepdims=True)
    hit = cols == down
    tile = jnp.max(jnp.where(hit, across, 0), axis=1, keepdims=True)
    tile_row = jnp.clip(jnp.max(jnp.where(hit, rows, 0), axis=1, keepdims=True), 0, row_count - 1)
    ordered = jnp.clip(
        jnp.max(jnp.where(rank == down, cols, 0), axis=1, keepdims=True), 0, col_count - 1
    )
    lane = lax.broadcasted_iota(jnp.int32, lists.shape, 1)
    lists[...] = jnp.where(lane == 0, tile, jnp.where(lane == 1, tile_row, ordered))


def kernel(
    nr, nc, total_rows, total_cols,
    rows_hbm, cols_hbm, tiles_hbm, u_hbm, expo_hbm, v_hbm, prior_hbm,
    u_out, v_out, vf_out, uf_out,
    rows_in, cols_in, tiles, u, expo, v, prior, lists, idx, in_sem,
    u2, part, got, gotz, own, pt, prods, terms, got_terms, g1c, g1q, g1z, g2c, g2q, g2z, qt, pair_ref,
    rs_send, rs_recv, z_send, z_recv, az_send, az_recv, ag_send, ag_recv,
    t_send, t_recv, c1_send, c1_recv, q1_send, q1_recv, z1_send, z1_recv,
    c2_send, c2_recv, q2_send, q2_recv, z2_send, z2_recv,
):
    nz = nr // QUADS
    width = u.shape[0]
    half = width // 2
    rt = terms.shape[0]
    rtc = rt // nc
    tp = part.shape[3]
    each = tiles.shape[0] // rt
    me = lax.axis_index("row")
    mc = lax.axis_index("col")
    z = me // QUADS
    gi = me % QUADS
    gx = gi + 1 - 2 * (gi % 2)
    gy = gi + 2 - 4 * (gi // 2)
    gd = (QUADS - 1) - gi
    base = z * QUADS
    to_x = {"row": base + gx}
    to_y = {"row": base + gy}
    to_d = {"row": base + gd}

    def to_z(zz):
        return {"row": zz * QUADS + gi}

    def to_c(cc):
        return {"col": cc}

    pending = []

    def remote(src, dst, ssem, rsem, dev):
        return pltpu.make_async_remote_copy(
            src_ref=src, dst_ref=dst, send_sem=ssem, recv_sem=rsem, device_id=dev,
            device_id_type=pl.DeviceIdType.MESH,
        )

    def send(*a):
        c = remote(*a)
        c.start()
        pending.append(c)

    fetch = [
        pltpu.make_async_copy(src, dst, in_sem.at[i])
        for i, (src, dst) in enumerate((
            (rows_hbm, rows_in), (cols_hbm, cols_in), (u_hbm, u), (tiles_hbm, tiles),
            (expo_hbm, expo), (v_hbm, v), (prior_hbm, prior),
        ))
    ]
    for c in fetch:
        c.start()
    barrier = pltpu.get_barrier_semaphore()
    peers = [to_x, to_y, to_d]
    peers += [to_z((z + k) % nz) for k in range(1, nz)]
    peers += [to_c((mc + k) % nc) for k in range(1, nc)]
    for p in peers:
        pl.semaphore_signal(barrier, inc=1, device_id=p, device_id_type=pl.DeviceIdType.MESH)

    for c in fetch[:2]:
        c.wait()
    tile_lists(rows_in, cols_in, lists, rt, expo.shape[0])
    to_scalars = pltpu.make_async_copy(lists, idx, in_sem.at[len(fetch)])
    to_scalars.start()
    fetch[2].wait()
    for r in range(rt):
        hi, lo = split(u[:, r * TL : (r + 1) * TL])
        u2[r, 0:width] = hi
        u2[r, width : 2 * width] = lo

    to_scalars.wait()
    for c in fetch[3:]:
        c.wait()

    def left_tile(j):
        th, tl_ = split(tiles[idx[j, 0]])
        both = jnp.concatenate([th, tl_], axis=1)
        x = jnp.dot(u2[idx[j, 1]], both, preferred_element_type=F32)
        y = x[:width] + x[width:]
        return y[:, :TL] + y[:, TL:]

    def compute(k):
        zz = (z + 1 + k) % nz
        for n, q in enumerate((gd, gx, gy, gi)):
            def body(t, _, q=q):
                y = left_tile((zz * QUADS + q) * tp + t)
                part[zz, q, 0, t] = y[:half]
                part[zz, q, 1, t] = y[half:]
                return 0
            lax.fori_loop(0, tp, body, 0, unroll=True)
            if n == 0 and k == 0:
                pl.semaphore_wait(barrier, len(peers))
            if n == 0:
                send(part.at[zz, q, 0], got.at[k, 0], rs_send.at[k, 0], rs_recv.at[k, 0], to_x)
                send(part.at[zz, q, 1], got.at[k, 1], rs_send.at[k, 1], rs_recv.at[k, 1], to_y)
            elif n == 1:
                send(part.at[zz, q, 0], got.at[k, 2], rs_send.at[k, 2], rs_recv.at[k, 2], to_x)
            elif n == 2:
                send(part.at[zz, q, 1], got.at[k, 3], rs_send.at[k, 3], rs_recv.at[k, 3], to_y)

    def rs_wait(k, n):
        remote(got.at[k, n], got.at[k, n], rs_send.at[k, n], rs_recv.at[k, n], to_x).wait_recv()

    def step2(k):
        zz = (z + 1 + k) % nz
        rs_wait(k, 0)
        part[zz, gy, 0] = part[zz, gy, 0] + got[k, 0]
        send(part.at[zz, gy, 0], got.at[k, 4], rs_send.at[k, 4], rs_recv.at[k, 4], to_y)
        rs_wait(k, 1)
        part[zz, gx, 1] = part[zz, gx, 1] + got[k, 1]
        send(part.at[zz, gx, 1], got.at[k, 5], rs_send.at[k, 5], rs_recv.at[k, 5], to_x)

    def step3(k):
        zz = (z + 1 + k) % nz
        for n in (2, 3, 4, 5):
            rs_wait(k, n)
        part[zz, gi, 0] = part[zz, gi, 0] + (got[k, 2] + got[k, 4])
        part[zz, gi, 1] = part[zz, gi, 1] + (got[k, 3] + got[k, 5])
        if k < nz - 1:
            send(part.at[zz, gi], gotz.at[z], z_send.at[k], z_recv.at[z], to_z(zz))

    for k in range(nz + 2):
        if k < nz:
            compute(k)
        if k == 0:
            tri = lax.broadcasted_iota(jnp.int32, prior.shape, 0) >= lax.broadcasted_iota(
                jnp.int32, prior.shape, 1
            )
            low = jnp.where(tri, prior[...], 0.0)
            own[...] = jnp.dot(low, v[...], precision=HIGH, preferred_element_type=F32)
        if 1 <= k < nz + 1:
            step2(k - 1)
        if 2 <= k:
            step3(k - 2)

    def scale_of(j):
        e = expo[j]
        return jnp.where(e % 2 == 1, 0.5, 1.0) * jnp.where(e >= 2, 0.25, 1.0)

    for k in range(1, nz):
        zs = (z + k) % nz
        remote(gotz.at[zs], gotz.at[zs], z_send.at[k - 1], z_recv.at[zs], to_z(zs)).wait_recv()
    for t in range(tp):
        sc = scale_of(me * tp + t)
        for h in range(2):
            x = part[z, gi, h, t]
            for k in range(1, nz):
                x = x + gotz[(z + k) % nz, h, t]
            pt[z, gi, h, t] = x * sc - own[h * half : (h + 1) * half, t * TL : (t + 1) * TL]

    for k in range(1, nz):
        zs = (z + k) % nz
        send(pt.at[z, gi], pt.at[z, gi], az_send.at[k - 1], az_recv.at[z], to_z(zs))

    def ag(src, k, n, dev):
        send(src, src, ag_send.at[k, n], ag_recv.at[k, n], dev)

    def ag_wait(dst, k, n):
        remote(dst, dst, ag_send.at[k, n], ag_recv.at[k, n], to_x).wait_recv()

    def right_tiles(zz, q):
        for t in range(tp):
            j = (zz * QUADS + q) * tp + t
            x = jnp.concatenate([pt[zz, q, 0, t], pt[zz, q, 1, t]], axis=0)
            xs = jnp.concatenate(split(x * scale_of(j)), axis=0)
            both = jnp.concatenate(split(tiles[idx[j, 0]]), axis=0)
            y = lax.dot_general(xs, both, (((1,), (1,)), ((), ())), preferred_element_type=F32)
            y = y[:width] + y[width:]
            prods[j] = y[:, :TL] + y[:, TL:]

    def gram_of(parts):
        acc = jnp.zeros((2 * width, 2 * width), F32)
        for x in parts:
            xx = jnp.concatenate(split(x), axis=0)
            acc = acc + lax.dot_general(
                xx, xx, (((1,), (1,)), ((), ())), preferred_element_type=F32
            )
        return pack(fold(acc))

    def own_tile(t):
        return jnp.concatenate([pt[z, gi, 0, t], pt[z, gi, 1, t]], axis=0)

    def arrive(k):
        zs = (z + nz - k) % nz
        if k:
            remote(pt.at[zs, gi], pt.at[zs, gi], az_send.at[0], az_recv.at[zs], to_z(zs)).wait_recv()
        ag(pt.at[zs, gi, 0], k, 0, to_y)
        ag(pt.at[zs, gi, 1], k, 1, to_x)
        ag(pt.at[zs, gi, 0], k, 2, to_x)
        ag(pt.at[zs, gi, 1], k, 3, to_y)
        right_tiles(zs, gi)

    def relay(k):
        zs = (z + nz - k) % nz
        ag_wait(pt.at[zs, gy, 0], k, 0)
        ag(pt.at[zs, gy, 0], k, 4, to_x)
        ag_wait(pt.at[zs, gx, 1], k, 1)
        ag(pt.at[zs, gx, 1], k, 5, to_y)

    def finish(k):
        zs = (z + nz - k) % nz
        ag_wait(pt.at[zs, gx, 0], k, 2)
        right_tiles(zs, gx)
        ag_wait(pt.at[zs, gy, 1], k, 3)
        right_tiles(zs, gy)
        ag_wait(pt.at[zs, gd, 0], k, 4)
        ag_wait(pt.at[zs, gd, 1], k, 5)
        right_tiles(zs, gd)

    def sum_start(buf, mine, n, x, ssem, rsem, to):
        buf[mine] = x
        for k in range(1, n):
            send(buf.at[mine], buf.at[mine], ssem.at[k - 1], rsem.at[mine], to((mine + k) % n))

    def sum_end(buf, mine, n, ssem, rsem, to):
        for k in range(1, n):
            o = (mine + k) % n
            remote(buf.at[o], buf.at[o], ssem.at[k - 1], rsem.at[o], to(o)).wait_recv()
        y = buf[0]
        for o in range(1, n):
            y = y + buf[o]
        return y

    def to_q(q):
        return {"row": base + q}

    first = (
        (g1c, mc, nc, c1_send, c1_recv, to_c),
        (g1q, gi, QUADS, q1_send, q1_recv, to_q),
        (g1z, z, nz, z1_send, z1_recv, to_z),
    )
    second = (
        (g2c, mc, nc, c2_send, c2_recv, to_c),
        (g2q, gi, QUADS, q2_send, q2_recv, to_q),
        (g2z, z, nz, z2_send, z2_recv, to_z),
    )

    def start(stage, x):
        buf, mine, n, ssem, rsem, to = stage
        sum_start(buf, mine, n, x, ssem, rsem, to)

    def end(stage):
        buf, mine, n, ssem, rsem, to = stage
        return sum_end(buf, mine, n, ssem, rsem, to)

    def first_factor():
        pair = factor_pair(unpack(end(first[2]) * (1.0 / total_cols)))
        pair_ref[...] = pair
        vf_out[...] = transpose_left(pair)
        for t in range(tp):
            x = jnp.concatenate([jnp.zeros((width, TL), F32), own_tile(t)], axis=0)
            v_out[:, t * TL : (t + 1) * TL] = jnp.dot(
                pair, x, precision=HIGH, preferred_element_type=F32
            )

    for k in range(nz + 2):
        if k < nz:
            arrive(k)
        if 1 <= k < nz + 1:
            relay(k - 1)
        if 2 <= k:
            finish(k - 2)
        if k == 0:
            start(first[0], gram_of(own_tile(t) for t in range(tp)))
        elif k == 1:
            start(first[1], end(first[0]))
        elif k == 2:
            start(first[2], end(first[1]))
        elif k == max(3, nz - 1):
            first_factor()

    def row_terms(r, _):
        x = prods[idx[r * each, 2]]
        for i in range(1, each):
            x = x + prods[idx[r * each + i, 2]]
        terms[r] = x
        return 0
    lax.fori_loop(0, rt, row_terms, 0)
    for k in range(1, nc):
        cc = (mc + k) % nc
        send(terms.at[pl.ds(cc * rtc, rtc)], got_terms.at[mc], t_send.at[k - 1], t_recv.at[mc], to_c(cc))

    for k in range(1, nc):
        cc = (mc + k) % nc
        remote(got_terms.at[cc], got_terms.at[cc], t_send.at[k - 1], t_recv.at[cc], to_c(cc)).wait_recv()
    root = math.sqrt(total_rows / total_cols)

    pair = pair_ref[...]
    for i in range(rtc):
        r = mc * rtc + i
        x = terms[r]
        for k in range(1, nc):
            x = x + got_terms[(mc + k) % nc, i]
        uu = u[:, pl.ds(pl.multiple_of(r * TL, TL), TL)]
        qt[i] = jnp.dot(
            pair, jnp.concatenate([-uu, root * x], axis=0), precision=HIGH, preferred_element_type=F32
        )
    x = gram_of(qt[i] for i in range(rtc))
    for stage in second:
        start(stage, x)
        x = end(stage)
    pair2 = factor_pair(unpack(x * (1.0 / total_rows)))
    uf_out[...] = transpose_left(pair2)
    for i in range(rtc):
        y = jnp.concatenate([jnp.zeros((width, TL), F32), qt[i]], axis=0)
        u_out[:, i * TL : (i + 1) * TL] = jnp.dot(
            pair2, y, precision=HIGH, preferred_element_type=F32
        )
    for c in pending:
        c.wait_send()


def hand_out(*refs):
    src, dst, sem = refs[:4], refs[4:8], refs[8]
    copies = [pltpu.make_async_copy(src[i], dst[i], sem.at[i]) for i in range(4)]
    for c in copies:
        c.start()
    for c in copies:
        c.wait()


def per_device(tiles, tile_rows, tile_cols, exponents, u_basis, v_basis, prior):
    nr, nc = lax.axis_size("row"), lax.axis_size("col")
    nz = nr // QUADS
    local = tiles[0, 0]
    rows, cols = tile_rows[0], tile_cols[0]
    count = local.shape[0]
    width, block_rows = u_basis.shape
    block_cols = exponents.shape[0]
    rt, ct = block_rows // TL, block_cols // TL
    tp = ct // nr
    rtc = rt // nc
    half = width // 2
    expo = exponents.reshape(ct, 1, TL)
    dma = pltpu.SemaphoreType.DMA
    vm = pl.BlockSpec(memory_space=pltpu.VMEM)

    def sems(*shape):
        return [dma(shape), dma(shape)]

    outs = pl.pallas_call(
        functools.partial(kernel, nr, nc, block_rows * nr, block_cols * nc),
        out_shape=(
            jax.ShapeDtypeStruct((width, block_rows // nc), F32),
            jax.ShapeDtypeStruct((width, block_cols // nr), F32),
            jax.ShapeDtypeStruct((width, width), F32),
            jax.ShapeDtypeStruct((width, width), F32),
        ),
        in_specs=[pl.BlockSpec(memory_space=pl.ANY)] * 7,
        out_specs=(vm,) * 4,
        scratch_shapes=[
            pltpu.VMEM((1, count), jnp.int32),
            pltpu.VMEM((1, count), jnp.int32),
            pltpu.VMEM((count, TL, TL), F32),
            pltpu.VMEM((width, block_rows), F32),
            pltpu.VMEM((ct, 1, TL), jnp.int32),
            pltpu.VMEM((width, tp * TL), F32),
            pltpu.VMEM((width, width), F32),
            pltpu.VMEM((count, TL), jnp.int32),
            pltpu.SMEM((count, TL), jnp.int32),
            dma((8,)),
            pltpu.VMEM((rt, 2 * width, TL), BF16),
            pltpu.VMEM((nz, QUADS, 2, tp, half, TL), F32),
            pltpu.VMEM((nz, 6, tp, half, TL), F32),
            pltpu.VMEM((nz, 2, tp, half, TL), F32),
            pltpu.VMEM((width, tp * TL), F32),
            pltpu.VMEM((nz, QUADS, 2, tp, half, TL), F32),
            pltpu.VMEM((ct, width, TL), F32),
            pltpu.VMEM((rt, width, TL), F32),
            pltpu.VMEM((nc, rtc, width, TL), F32),
            *[pltpu.VMEM((n, half, 2 * width), F32) for n in (nc, QUADS, nz)] * 2,
            pltpu.VMEM((rtc, width, TL), F32),
            pltpu.VMEM((width, 2 * width), F32),
            *sems(nz, 6),
            dma((nz,)), dma((nz,)),
            dma((nz,)), dma((nz,)),
            *sems(nz, 6),
            *sems(nc),
            *[x for n in (nc, QUADS, nz) for x in sems(n)] * 2,
        ],
        compiler_params=pltpu.CompilerParams(
            collective_id=0, has_side_effects=True, vmem_limit_bytes=56 * 1024 * 1024
        ),
    )(rows, cols, local, u_basis, expo, v_basis, prior)
    return pl.pallas_call(
        hand_out,
        out_shape=tuple(jax.ShapeDtypeStruct(o.shape, o.dtype) for o in outs),
        in_specs=[pl.BlockSpec(memory_space=pl.ANY)] * 4,
        out_specs=(pl.BlockSpec(memory_space=pl.ANY),) * 4,
        scratch_shapes=[dma((4,))],
    )(*outs)


def solution(mesh):
    placed = (
        P("row", "col", None, None, None),
        P("row", "col", None),
        P("row", "col", None),
        P("col"),
        P(None, "row"),
        P(None, ("col", "row")),
        P(),
    )
    return jax.shard_map(
        per_device,
        mesh=mesh,
        in_specs=placed,
        out_specs=(P(None, ("row", "col")), P(None, ("col", "row")), P(), P()),
        check_vma=False,
    )
```

```python
import functools
import math

import jax
import jax.numpy as jnp
from jax import lax
from jax.experimental import pallas as pl
from jax.experimental.pallas import tpu as pltpu
from jax.sharding import PartitionSpec as P

F32 = jnp.float32
BF16 = jnp.bfloat16
HIGH = lax.Precision.HIGHEST
TL = 128
QUADS = 4


def split(x):
    hi = x.astype(BF16)
    return hi, (x - hi.astype(F32)).astype(BF16)


def fold(x):
    w = x.shape[0] // 2
    y = x[:w] + x[w:]
    return y + pltpu.roll(y, w, 1)


def pack(x):
    w = x.shape[0]
    lane = lax.broadcasted_iota(jnp.int32, (w // 2, 2 * w), 1)
    return jnp.where(lane < w, x[: w // 2], x[w // 2 :])


def unpack(x):
    w = x.shape[1] // 2
    lane = lax.broadcasted_iota(jnp.int32, x.shape, 1)
    y = pltpu.roll(x, w, 1)
    return jnp.concatenate([jnp.where(lane < w, x, y), jnp.where(lane < w, y, x)], axis=0)


class Elimination:
    def __init__(self, gram2):
        w = gram2.shape[0]
        self.row = lax.broadcasted_iota(jnp.int32, (w, 2 * w), 0)
        self.lane = lax.broadcasted_iota(jnp.int32, (w, 2 * w), 1)
        unit = jnp.where(self.lane - w == self.row, 1.0, 0.0).astype(F32)
        self.m = jnp.where(self.lane < w, gram2, unit)
        self.done, self.top, self.width = [], 0, w

    def steps(self, begin, end, block=4):
        m, top = self.m, self.top
        for j in range(begin, end, block):
            o = j - top
            below = self.row[top:]
            cols = [jnp.broadcast_to(m[:, j + i : j + i + 1], m.shape) for i in range(block)]
            rows = [m[o + i : o + i + 1] for i in range(block)]
            a = {(i, l): cols[l][o + i : o + i + 1] for i in range(block) for l in range(i, block)}
            for i in range(block):
                inv = 1.0 / a[i, i]
                m = m - jnp.where(below > j + i, cols[i], 0.0) * (rows[i] * inv)
                for l in range(i + 1, block):
                    s = a[i, l] * inv
                    rows[l] = rows[l] - s * rows[i]
                    cols[l] = cols[l] - s * cols[i]
                    for q in range(l, block):
                        a[l, q] = a[l, q] - s * a[i, q]
            if (j + block) % 8 == 0:
                self.done.append(m[:8])
                m = m[8:]
                top += 8
        self.m, self.top = m, top

    def pair(self):
        row, lane, w = self.row, self.lane, self.width
        m = jnp.concatenate(self.done, axis=0)
        diag = jnp.sum(jnp.where(lane == row, m, 0.0), axis=1, keepdims=True)
        m = m * (1.0 / jnp.sqrt(diag))
        return jnp.where((lane >= w) | (lane >= row), m, 0.0)


def factor_pair(gram2):
    e = Elimination(gram2)
    e.steps(0, gram2.shape[0])
    return e.pair()


def transpose_left(pair):
    w = pair.shape[0]
    return jnp.concatenate([pair, pair], axis=0).T[:w, :w]


def tile_lists(rows_in, cols_in, lists, row_count, col_count):
    n = rows_in.shape[1]
    rows = jnp.broadcast_to(rows_in[...], (n, n))
    cols = jnp.broadcast_to(cols_in[...], (n, n))
    down = lax.broadcasted_iota(jnp.int32, (n, n), 0)
    across = lax.broadcasted_iota(jnp.int32, (n, n), 1)
    key = rows * n + across
    key_down = jnp.sum(jnp.where(down == across, key, 0), axis=1, keepdims=True)
    rank = jnp.sum(jnp.where(key_down < key, 1, 0), axis=0, keepdims=True)
    hit = cols == down
    tile = jnp.max(jnp.where(hit, across, 0), axis=1, keepdims=True)
    tile_row = jnp.clip(jnp.max(jnp.where(hit, rows, 0), axis=1, keepdims=True), 0, row_count - 1)
    ordered = jnp.clip(
        jnp.max(jnp.where(rank == down, cols, 0), axis=1, keepdims=True), 0, col_count - 1
    )
    lane = lax.broadcasted_iota(jnp.int32, lists.shape, 1)
    lists[...] = jnp.where(lane == 0, tile, jnp.where(lane == 1, tile_row, ordered))


def kernel(
    nr, nc, total_rows, total_cols,
    rows_hbm, cols_hbm, tiles_hbm, u_hbm, expo_hbm, v_hbm, prior_hbm,
    u_out, v_out, vf_out, uf_out,
    rows_in, cols_in, tiles, u, expo, v, prior, lists, idx, in_sem,
    u2, part, got, gotz, own, pt, prods, terms, got_terms, g1c, g1q, g1z, g2c, g2q, g2z, qt, pair_ref,
    rs_send, rs_recv, z_send, z_recv, az_send, az_recv, ag_send, ag_recv,
    t_send, t_recv, c1_send, c1_recv, q1_send, q1_recv, z1_send, z1_recv,
    c2_send, c2_recv, q2_send, q2_recv, z2_send, z2_recv,
):
    nz = nr // QUADS
    width = u.shape[0]
    half = width // 2
    rt = terms.shape[0]
    rtc = rt // nc
    tp = part.shape[3]
    each = tiles.shape[0] // rt
    me = lax.axis_index("row")
    mc = lax.axis_index("col")
    z = me // QUADS
    gi = me % QUADS
    gx = gi + 1 - 2 * (gi % 2)
    gy = gi + 2 - 4 * (gi // 2)
    gd = (QUADS - 1) - gi
    base = z * QUADS
    to_x = {"row": base + gx}
    to_y = {"row": base + gy}
    to_d = {"row": base + gd}

    def to_z(zz):
        return {"row": zz * QUADS + gi}

    def to_c(cc):
        return {"col": cc}

    pending = []

    def remote(src, dst, ssem, rsem, dev):
        return pltpu.make_async_remote_copy(
            src_ref=src, dst_ref=dst, send_sem=ssem, recv_sem=rsem, device_id=dev,
            device_id_type=pl.DeviceIdType.MESH,
        )

    def send(*a):
        c = remote(*a)
        c.start()
        pending.append(c)

    fetch = [
        pltpu.make_async_copy(src, dst, in_sem.at[i])
        for i, (src, dst) in enumerate((
            (rows_hbm, rows_in), (cols_hbm, cols_in), (u_hbm, u), (tiles_hbm, tiles),
            (expo_hbm, expo), (v_hbm, v), (prior_hbm, prior),
        ))
    ]
    for c in fetch:
        c.start()
    barrier = pltpu.get_barrier_semaphore()
    peers = [to_x, to_y, to_d]
    peers += [to_z((z + k) % nz) for k in range(1, nz)]
    peers += [to_c((mc + k) % nc) for k in range(1, nc)]
    for p in peers:
        pl.semaphore_signal(barrier, inc=1, device_id=p, device_id_type=pl.DeviceIdType.MESH)

    for c in fetch[:2]:
        c.wait()
    tile_lists(rows_in, cols_in, lists, rt, expo.shape[0])
    to_scalars = pltpu.make_async_copy(lists, idx, in_sem.at[len(fetch)])
    to_scalars.start()
    fetch[2].wait()
    for r in range(rt):
        hi, lo = split(u[:, r * TL : (r + 1) * TL])
        u2[r, 0:width] = hi
        u2[r, width : 2 * width] = lo

    to_scalars.wait()
    for c in fetch[3:]:
        c.wait()

    def left_tile(j):
        th, tl_ = split(tiles[idx[j, 0]])
        both = jnp.concatenate([th, tl_], axis=1)
        x = jnp.dot(u2[idx[j, 1]], both, preferred_element_type=F32)
        y = x[:width] + x[width:]
        return y[:, :TL] + y[:, TL:]

    def compute(k):
        zz = (z + 1 + k) % nz
        for n, q in enumerate((gd, gx, gy, gi)):
            def body(t, _, q=q):
                y = left_tile((zz * QUADS + q) * tp + t)
                part[zz, q, 0, t] = y[:half]
                part[zz, q, 1, t] = y[half:]
                return 0
            lax.fori_loop(0, tp, body, 0, unroll=True)
            if n == 0 and k == 0:
                pl.semaphore_wait(barrier, len(peers))
            if n == 0:
                send(part.at[zz, q, 0], got.at[k, 0], rs_send.at[k, 0], rs_recv.at[k, 0], to_x)
                send(part.at[zz, q, 1], got.at[k, 1], rs_send.at[k, 1], rs_recv.at[k, 1], to_y)
            elif n == 1:
                send(part.at[zz, q, 0], got.at[k, 2], rs_send.at[k, 2], rs_recv.at[k, 2], to_x)
            elif n == 2:
                send(part.at[zz, q, 1], got.at[k, 3], rs_send.at[k, 3], rs_recv.at[k, 3], to_y)

    def rs_wait(k, n):
        remote(got.at[k, n], got.at[k, n], rs_send.at[k, n], rs_recv.at[k, n], to_x).wait_recv()

    def step2(k):
        zz = (z + 1 + k) % nz
        rs_wait(k, 0)
        part[zz, gy, 0] = part[zz, gy, 0] + got[k, 0]
        send(part.at[zz, gy, 0], got.at[k, 4], rs_send.at[k, 4], rs_recv.at[k, 4], to_y)
        rs_wait(k, 1)
        part[zz, gx, 1] = part[zz, gx, 1] + got[k, 1]
        send(part.at[zz, gx, 1], got.at[k, 5], rs_send.at[k, 5], rs_recv.at[k, 5], to_x)

    def step3(k):
        zz = (z + 1 + k) % nz
        for n in (2, 3, 4, 5):
            rs_wait(k, n)
        part[zz, gi, 0] = part[zz, gi, 0] + (got[k, 2] + got[k, 4])
        part[zz, gi, 1] = part[zz, gi, 1] + (got[k, 3] + got[k, 5])
        if k < nz - 1:
            send(part.at[zz, gi], gotz.at[z], z_send.at[k], z_recv.at[z], to_z(zz))

    for k in range(nz + 2):
        if k < nz:
            compute(k)
        if k == 0:
            tri = lax.broadcasted_iota(jnp.int32, prior.shape, 0) >= lax.broadcasted_iota(
                jnp.int32, prior.shape, 1
            )
            low = jnp.where(tri, prior[...], 0.0)
            own[...] = jnp.dot(low, v[...], precision=HIGH, preferred_element_type=F32)
        if 1 <= k < nz + 1:
            step2(k - 1)
        if 2 <= k:
            step3(k - 2)

    def scale_of(j):
        e = expo[j]
        return jnp.where(e % 2 == 1, 0.5, 1.0) * jnp.where(e >= 2, 0.25, 1.0)

    for k in range(1, nz):
        zs = (z + k) % nz
        remote(gotz.at[zs], gotz.at[zs], z_send.at[k - 1], z_recv.at[zs], to_z(zs)).wait_recv()
    for t in range(tp):
        sc = scale_of(me * tp + t)
        for h in range(2):
            x = part[z, gi, h, t]
            for k in range(1, nz):
                x = x + gotz[(z + k) % nz, h, t]
            pt[z, gi, h, t] = x * sc - own[h * half : (h + 1) * half, t * TL : (t + 1) * TL]

    def spread(k):
        if 1 <= k < nz:
            zs = (z + k) % nz
            send(pt.at[z, gi], pt.at[z, gi], az_send.at[k - 1], az_recv.at[z], to_z(zs))

    def ag(src, k, n, dev):
        send(src, src, ag_send.at[k, n], ag_recv.at[k, n], dev)

    def ag_wait(dst, k, n):
        remote(dst, dst, ag_send.at[k, n], ag_recv.at[k, n], to_x).wait_recv()

    def right_tiles(zz, q):
        for t in range(tp):
            j = (zz * QUADS + q) * tp + t
            x = jnp.concatenate([pt[zz, q, 0, t], pt[zz, q, 1, t]], axis=0)
            xs = jnp.concatenate(split(x * scale_of(j)), axis=0)
            both = jnp.concatenate(split(tiles[idx[j, 0]]), axis=0)
            y = lax.dot_general(xs, both, (((1,), (1,)), ((), ())), preferred_element_type=F32)
            y = y[:width] + y[width:]
            prods[j] = y[:, :TL] + y[:, TL:]

    def gram_of(parts):
        acc = jnp.zeros((2 * width, 2 * width), F32)
        for x in parts:
            xx = jnp.concatenate(split(x), axis=0)
            acc = acc + lax.dot_general(
                xx, xx, (((1,), (1,)), ((), ())), preferred_element_type=F32
            )
        return pack(fold(acc))

    def own_tile(t):
        return jnp.concatenate([pt[z, gi, 0, t], pt[z, gi, 1, t]], axis=0)

    def arrive(k):
        zs = (z + nz - k) % nz
        if k:
            remote(pt.at[zs, gi], pt.at[zs, gi], az_send.at[0], az_recv.at[zs], to_z(zs)).wait_recv()
        spread(k + 1)
        ag(pt.at[zs, gi, 0], k, 0, to_y)
        ag(pt.at[zs, gi, 1], k, 1, to_x)
        ag(pt.at[zs, gi, 0], k, 2, to_x)
        ag(pt.at[zs, gi, 1], k, 3, to_y)
        right_tiles(zs, gi)

    def relay(k):
        zs = (z + nz - k) % nz
        ag_wait(pt.at[zs, gy, 0], k, 0)
        ag(pt.at[zs, gy, 0], k, 4, to_x)
        ag_wait(pt.at[zs, gx, 1], k, 1)
        ag(pt.at[zs, gx, 1], k, 5, to_y)

    def finish(k):
        zs = (z + nz - k) % nz
        ag_wait(pt.at[zs, gx, 0], k, 2)
        right_tiles(zs, gx)
        ag_wait(pt.at[zs, gy, 1], k, 3)
        right_tiles(zs, gy)
        ag_wait(pt.at[zs, gd, 0], k, 4)
        ag_wait(pt.at[zs, gd, 1], k, 5)
        right_tiles(zs, gd)

    def sum_start(buf, mine, n, x, ssem, rsem, to):
        buf[mine] = x
        for k in range(1, n):
            send(buf.at[mine], buf.at[mine], ssem.at[k - 1], rsem.at[mine], to((mine + k) % n))

    def sum_end(buf, mine, n, ssem, rsem, to):
        for k in range(1, n):
            o = (mine + k) % n
            remote(buf.at[o], buf.at[o], ssem.at[k - 1], rsem.at[o], to(o)).wait_recv()
        y = buf[0]
        for o in range(1, n):
            y = y + buf[o]
        return y

    def to_q(q):
        return {"row": base + q}

    first = (
        (g1c, mc, nc, c1_send, c1_recv, to_c),
        (g1q, gi, QUADS, q1_send, q1_recv, to_q),
        (g1z, z, nz, z1_send, z1_recv, to_z),
    )
    second = (
        (g2c, mc, nc, c2_send, c2_recv, to_c),
        (g2q, gi, QUADS, q2_send, q2_recv, to_q),
        (g2z, z, nz, z2_send, z2_recv, to_z),
    )

    def start(stage, x):
        buf, mine, n, ssem, rsem, to = stage
        sum_start(buf, mine, n, x, ssem, rsem, to)

    def end(stage):
        buf, mine, n, ssem, rsem, to = stage
        return sum_end(buf, mine, n, ssem, rsem, to)

    def first_factor(elim):
        elim.steps(width // 2, width)
        pair = elim.pair()
        pair_ref[...] = pair
        vf_out[...] = transpose_left(pair)
        for t in range(tp):
            x = jnp.concatenate([jnp.zeros((width, TL), F32), own_tile(t)], axis=0)
            v_out[:, t * TL : (t + 1) * TL] = jnp.dot(
                pair, x, precision=HIGH, preferred_element_type=F32
            )

    for k in range(nz + 2):
        if k < nz:
            arrive(k)
        if 1 <= k < nz + 1:
            relay(k - 1)
        if k == max(4, nz):
            first_factor(elim)
        if 2 <= k:
            finish(k - 2)
        if k == 0:
            start(first[0], gram_of(own_tile(t) for t in range(tp)))
        elif k == 1:
            start(first[1], end(first[0]))
        elif k == 2:
            start(first[2], end(first[1]))
        elif k == max(3, nz - 1):
            elim = Elimination(unpack(end(first[2]) * (1.0 / total_cols)))
            elim.steps(0, width // 2)

    def row_terms(r, _):
        x = prods[idx[r * each, 2]]
        for i in range(1, each):
            x = x + prods[idx[r * each + i, 2]]
        terms[r] = x
        return 0
    lax.fori_loop(0, rt, row_terms, 0)
    for k in range(1, nc):
        cc = (mc + k) % nc
        send(terms.at[pl.ds(cc * rtc, rtc)], got_terms.at[mc], t_send.at[k - 1], t_recv.at[mc], to_c(cc))

    for k in range(1, nc):
        cc = (mc + k) % nc
        remote(got_terms.at[cc], got_terms.at[cc], t_send.at[k - 1], t_recv.at[cc], to_c(cc)).wait_recv()
    root = math.sqrt(total_rows / total_cols)

    pair = pair_ref[...]
    for i in range(rtc):
        r = mc * rtc + i
        x = terms[r]
        for k in range(1, nc):
            x = x + got_terms[(mc + k) % nc, i]
        uu = u[:, pl.ds(pl.multiple_of(r * TL, TL), TL)]
        qt[i] = jnp.dot(
            pair, jnp.concatenate([-uu, root * x], axis=0), precision=HIGH, preferred_element_type=F32
        )
    x = gram_of(qt[i] for i in range(rtc))
    for stage in second:
        start(stage, x)
        x = end(stage)
    pair2 = factor_pair(unpack(x * (1.0 / total_rows)))
    uf_out[...] = transpose_left(pair2)
    for i in range(rtc):
        y = jnp.concatenate([jnp.zeros((width, TL), F32), qt[i]], axis=0)
        u_out[:, i * TL : (i + 1) * TL] = jnp.dot(
            pair2, y, precision=HIGH, preferred_element_type=F32
        )
    for c in pending:
        c.wait_send()


def hand_out(*refs):
    for src, dst in zip(refs[:4], refs[4:]):
        dst[...] = src[...]


def per_device(tiles, tile_rows, tile_cols, exponents, u_basis, v_basis, prior):
    nr, nc = lax.axis_size("row"), lax.axis_size("col")
    nz = nr // QUADS
    local = tiles[0, 0]
    rows, cols = tile_rows[0], tile_cols[0]
    count = local.shape[0]
    width, block_rows = u_basis.shape
    block_cols = exponents.shape[0]
    rt, ct = block_rows // TL, block_cols // TL
    tp = ct // nr
    rtc = rt // nc
    half = width // 2
    expo = exponents.reshape(ct, 1, TL)
    dma = pltpu.SemaphoreType.DMA
    vm = pl.BlockSpec(memory_space=pltpu.VMEM)

    def sems(*shape):
        return [dma(shape), dma(shape)]

    outs = pl.pallas_call(
        functools.partial(kernel, nr, nc, block_rows * nr, block_cols * nc),
        out_shape=(
            jax.ShapeDtypeStruct((width, block_rows // nc), F32),
            jax.ShapeDtypeStruct((width, block_cols // nr), F32),
            jax.ShapeDtypeStruct((width, width), F32),
            jax.ShapeDtypeStruct((width, width), F32),
        ),
        in_specs=[pl.BlockSpec(memory_space=pl.ANY)] * 7,
        out_specs=(vm,) * 4,
        scratch_shapes=[
            pltpu.VMEM((1, count), jnp.int32),
            pltpu.VMEM((1, count), jnp.int32),
            pltpu.VMEM((count, TL, TL), F32),
            pltpu.VMEM((width, block_rows), F32),
            pltpu.VMEM((ct, 1, TL), jnp.int32),
            pltpu.VMEM((width, tp * TL), F32),
            pltpu.VMEM((width, width), F32),
            pltpu.VMEM((count, TL), jnp.int32),
            pltpu.SMEM((count, TL), jnp.int32),
            dma((8,)),
            pltpu.VMEM((rt, 2 * width, TL), BF16),
            pltpu.VMEM((nz, QUADS, 2, tp, half, TL), F32),
            pltpu.VMEM((nz, 6, tp, half, TL), F32),
            pltpu.VMEM((nz, 2, tp, half, TL), F32),
            pltpu.VMEM((width, tp * TL), F32),
            pltpu.VMEM((nz, QUADS, 2, tp, half, TL), F32),
            pltpu.VMEM((ct, width, TL), F32),
            pltpu.VMEM((rt, width, TL), F32),
            pltpu.VMEM((nc, rtc, width, TL), F32),
            *[pltpu.VMEM((n, half, 2 * width), F32) for n in (nc, QUADS, nz)] * 2,
            pltpu.VMEM((rtc, width, TL), F32),
            pltpu.VMEM((width, 2 * width), F32),
            *sems(nz, 6),
            dma((nz,)), dma((nz,)),
            dma((nz,)), dma((nz,)),
            *sems(nz, 6),
            *sems(nc),
            *[x for n in (nc, QUADS, nz) for x in sems(n)] * 2,
        ],
        compiler_params=pltpu.CompilerParams(
            collective_id=0, has_side_effects=True, vmem_limit_bytes=56 * 1024 * 1024
        ),
    )(rows, cols, local, u_basis, expo, v_basis, prior)
    return pl.pallas_call(
        hand_out,
        out_shape=tuple(jax.ShapeDtypeStruct(o.shape, o.dtype) for o in outs),
        in_specs=[vm] * 4,
        out_specs=(vm,) * 4,
    )(*outs)


def solution(mesh):
    placed = (
        P("row", "col", None, None, None),
        P("row", "col", None),
        P("row", "col", None),
        P("col"),
        P(None, "row"),
        P(None, ("col", "row")),
        P(),
    )
    return jax.shard_map(
        per_device,
        mesh=mesh,
        in_specs=placed,
        out_specs=(P(None, ("row", "col")), P(None, ("col", "row")), P(), P()),
        check_vma=False,
    )
```

```python
import functools
import math

import jax
import jax.numpy as jnp
from jax import lax
from jax.experimental import pallas as pl
from jax.experimental.pallas import tpu as pltpu
from jax.sharding import PartitionSpec as P

F32 = jnp.float32
BF16 = jnp.bfloat16
HIGH = lax.Precision.HIGHEST
TL = 128
QUADS = 4


def split(x):
    hi = x.astype(BF16)
    return hi, (x - hi.astype(F32)).astype(BF16)


def fold(x):
    w = x.shape[0] // 2
    y = x[:w] + x[w:]
    return y + pltpu.roll(y, w, 1)


def pack(x):
    w = x.shape[0]
    lane = lax.broadcasted_iota(jnp.int32, (w // 2, 2 * w), 1)
    return jnp.where(lane < w, x[: w // 2], x[w // 2 :])


def unpack(x):
    w = x.shape[1] // 2
    lane = lax.broadcasted_iota(jnp.int32, x.shape, 1)
    y = pltpu.roll(x, w, 1)
    return jnp.concatenate([jnp.where(lane < w, x, y), jnp.where(lane < w, y, x)], axis=0)


class Elimination:
    def __init__(self, gram2):
        w = gram2.shape[0]
        self.row = lax.broadcasted_iota(jnp.int32, (w, 2 * w), 0)
        self.lane = lax.broadcasted_iota(jnp.int32, (w, 2 * w), 1)
        unit = jnp.where(self.lane - w == self.row, 1.0, 0.0).astype(F32)
        self.m = jnp.where(self.lane < w, gram2, unit)
        self.done, self.top, self.width = [], 0, w

    def steps(self, begin, end, block=4):
        m, top = self.m, self.top
        for j in range(begin, end, block):
            o = j - top
            below = self.row[top:]
            cols = [jnp.broadcast_to(m[:, j + i : j + i + 1], m.shape) for i in range(block)]
            rows = [m[o + i : o + i + 1] for i in range(block)]
            a = {(i, l): cols[l][o + i : o + i + 1] for i in range(block) for l in range(i, block)}
            for i in range(block):
                inv = 1.0 / a[i, i]
                m = m - jnp.where(below > j + i, cols[i], 0.0) * (rows[i] * inv)
                for l in range(i + 1, block):
                    s = a[i, l] * inv
                    rows[l] = rows[l] - s * rows[i]
                    cols[l] = cols[l] - s * cols[i]
                    for q in range(l, block):
                        a[l, q] = a[l, q] - s * a[i, q]
            if (j + block) % 8 == 0:
                self.done.append(m[:8])
                m = m[8:]
                top += 8
        self.m, self.top = m, top

    def pair(self):
        row, lane, w = self.row, self.lane, self.width
        m = jnp.concatenate(self.done, axis=0)
        diag = jnp.sum(jnp.where(lane == row, m, 0.0), axis=1, keepdims=True)
        m = m * (1.0 / jnp.sqrt(diag))
        return jnp.where((lane >= w) | (lane >= row), m, 0.0)


def factor_pair(gram2):
    e = Elimination(gram2)
    e.steps(0, gram2.shape[0])
    return e.pair()


def transpose_left(pair):
    w = pair.shape[0]
    return jnp.concatenate([pair, pair], axis=0).T[:w, :w]


def tile_lists(rows_in, cols_in, lists, row_count, col_count):
    n = rows_in.shape[1]
    rows = jnp.broadcast_to(rows_in[...], (n, n))
    cols = jnp.broadcast_to(cols_in[...], (n, n))
    down = lax.broadcasted_iota(jnp.int32, (n, n), 0)
    across = lax.broadcasted_iota(jnp.int32, (n, n), 1)
    key = rows * n + across
    key_down = jnp.sum(jnp.where(down == across, key, 0), axis=1, keepdims=True)
    rank = jnp.sum(jnp.where(key_down < key, 1, 0), axis=0, keepdims=True)
    hit = cols == down
    tile = jnp.max(jnp.where(hit, across, 0), axis=1, keepdims=True)
    tile_row = jnp.clip(jnp.max(jnp.where(hit, rows, 0), axis=1, keepdims=True), 0, row_count - 1)
    ordered = jnp.clip(
        jnp.max(jnp.where(rank == down, cols, 0), axis=1, keepdims=True), 0, col_count - 1
    )
    lane = lax.broadcasted_iota(jnp.int32, lists.shape, 1)
    lists[...] = jnp.where(lane == 0, tile, jnp.where(lane == 1, tile_row, ordered))


def kernel(
    nr, nc, total_rows, total_cols,
    rows_hbm, cols_hbm, tiles_hbm, u_hbm, expo_hbm, v_hbm, prior_hbm,
    u_out, v_out, vf_out, uf_out,
    rows_in, cols_in, tiles, u, expo, v, prior, lists, idx, in_sem,
    u2, part, got, gotz, own, pt, prods, terms, got_terms, g1c, g1q, g1z, g2c, g2q, g2z, qt, pair_ref,
    rs_send, rs_recv, z_send, z_recv, az_send, az_recv, ag_send, ag_recv,
    t_send, t_recv, c1_send, c1_recv, q1_send, q1_recv, z1_send, z1_recv,
    c2_send, c2_recv, q2_send, q2_recv, z2_send, z2_recv,
):
    nz = nr // QUADS
    width = u.shape[0]
    half = width // 2
    rt = terms.shape[0]
    rtc = rt // nc
    ns, tps = part.shape[0], part.shape[4]
    tp = ns * tps
    each = tiles.shape[0] // rt
    me = lax.axis_index("row")
    mc = lax.axis_index("col")
    z = me // QUADS
    gi = me % QUADS
    gx = gi + 1 - 2 * (gi % 2)
    gy = gi + 2 - 4 * (gi // 2)
    gd = (QUADS - 1) - gi
    base = z * QUADS
    to_x = {"row": base + gx}
    to_y = {"row": base + gy}
    to_d = {"row": base + gd}

    def to_z(zz):
        return {"row": zz * QUADS + gi}

    def to_c(cc):
        return {"col": cc}

    pending = []

    def remote(src, dst, ssem, rsem, dev):
        return pltpu.make_async_remote_copy(
            src_ref=src, dst_ref=dst, send_sem=ssem, recv_sem=rsem, device_id=dev,
            device_id_type=pl.DeviceIdType.MESH,
        )

    def send(*a):
        c = remote(*a)
        c.start()
        pending.append(c)

    fetch = [
        pltpu.make_async_copy(src, dst, in_sem.at[i])
        for i, (src, dst) in enumerate((
            (rows_hbm, rows_in), (cols_hbm, cols_in), (u_hbm, u), (tiles_hbm, tiles),
            (expo_hbm, expo), (v_hbm, v), (prior_hbm, prior),
        ))
    ]
    for c in fetch:
        c.start()
    barrier = pltpu.get_barrier_semaphore()
    peers = [to_x, to_y, to_d]
    peers += [to_z((z + k) % nz) for k in range(1, nz)]
    peers += [to_c((mc + k) % nc) for k in range(1, nc)]
    for p in peers:
        pl.semaphore_signal(barrier, inc=1, device_id=p, device_id_type=pl.DeviceIdType.MESH)

    for c in fetch[:2]:
        c.wait()
    tile_lists(rows_in, cols_in, lists, rt, expo.shape[0])
    to_scalars = pltpu.make_async_copy(lists, idx, in_sem.at[len(fetch)])
    to_scalars.start()
    fetch[2].wait()
    for r in range(rt):
        hi, lo = split(u[:, r * TL : (r + 1) * TL])
        u2[r, 0:width] = hi
        u2[r, width : 2 * width] = lo

    to_scalars.wait()
    for c in fetch[3:]:
        c.wait()

    def left_tile(j):
        th, tl_ = split(tiles[idx[j, 0]])
        both = jnp.concatenate([th, tl_], axis=1)
        x = jnp.dot(u2[idx[j, 1]], both, preferred_element_type=F32)
        y = x[:width] + x[width:]
        return y[:, :TL] + y[:, TL:]

    def column(st, zz, q, t):
        return (zz * QUADS + q) * tp + st * tps + t

    def compute(st, k):
        zz = (z + 1 + k) % nz
        i = st * nz + k
        for n, q in enumerate((gd, gx, gy, gi)):
            for t in range(tps):
                y = left_tile(column(st, zz, q, t))
                part[st, zz, q, 0, t] = y[:half]
                part[st, zz, q, 1, t] = y[half:]
            if n == 0 and i == 0:
                pl.semaphore_wait(barrier, len(peers))
            if n == 0:
                rs(part.at[st, zz, q, 0], i, 0, to_x)
                rs(part.at[st, zz, q, 1], i, 1, to_y)
            elif n == 1:
                rs(part.at[st, zz, q, 0], i, 2, to_x)
            elif n == 2:
                rs(part.at[st, zz, q, 1], i, 3, to_y)

    def rs(src, i, n, dev):
        send(src, got.at[i, n], rs_send.at[i, n], rs_recv.at[i, n], dev)

    def rs_wait(i, n):
        remote(got.at[i, n], got.at[i, n], rs_send.at[i, n], rs_recv.at[i, n], to_x).wait_recv()

    def step2(st, k):
        zz = (z + 1 + k) % nz
        i = st * nz + k
        rs_wait(i, 0)
        part[st, zz, gy, 0] = part[st, zz, gy, 0] + got[i, 0]
        rs(part.at[st, zz, gy, 0], i, 4, to_y)
        rs_wait(i, 1)
        part[st, zz, gx, 1] = part[st, zz, gx, 1] + got[i, 1]
        rs(part.at[st, zz, gx, 1], i, 5, to_x)

    def step3(st, k):
        zz = (z + 1 + k) % nz
        i = st * nz + k
        for n in (2, 3, 4, 5):
            rs_wait(i, n)
        part[st, zz, gi, 0] = part[st, zz, gi, 0] + (got[i, 2] + got[i, 4])
        part[st, zz, gi, 1] = part[st, zz, gi, 1] + (got[i, 3] + got[i, 5])
        if k < nz - 1:
            send(part.at[st, zz, gi], gotz.at[st, z], z_send.at[st, k], z_recv.at[st, z], to_z(zz))

    def own_term():
        tri = lax.broadcasted_iota(jnp.int32, prior.shape, 0) >= lax.broadcasted_iota(
            jnp.int32, prior.shape, 1
        )
        low = jnp.where(tri, prior[...], 0.0)
        own[...] = jnp.dot(low, v[...], precision=HIGH, preferred_element_type=F32)

    def scale_of(j):
        e = expo[j]
        return jnp.where((e & 1) == 1, 0.5, 1.0) * jnp.where(e >= 2, 0.25, 1.0)

    def final(st):
        for k in range(1, nz):
            zs = (z + k) % nz
            remote(
                gotz.at[st, zs], gotz.at[st, zs], z_send.at[st, k - 1], z_recv.at[st, zs], to_z(zs)
            ).wait_recv()
        for t in range(tps):
            at = (st * tps + t) * TL
            sc = scale_of(column(st, z, gi, t))
            for h in range(2):
                x = part[st, z, gi, h, t]
                for k in range(1, nz):
                    x = x + gotz[st, (z + k) % nz, h, t]
                pt[st, z, gi, h, t] = x * sc - own[h * half : (h + 1) * half, at : at + TL]

    def spread(st, k):
        if 1 <= k < nz:
            zs = (z + k) % nz
            send(
                pt.at[st, z, gi], pt.at[st, z, gi], az_send.at[st, k - 1], az_recv.at[st, z], to_z(zs)
            )

    def ag(src, k, n, dev):
        send(src, src, ag_send.at[k, n], ag_recv.at[k, n], dev)

    def ag_wait(dst, k, n):
        remote(dst, dst, ag_send.at[k, n], ag_recv.at[k, n], to_x).wait_recv()

    def right_tiles(st, zz, q):
        for t in range(tps):
            j = column(st, zz, q, t)
            x = jnp.concatenate([pt[st, zz, q, 0, t], pt[st, zz, q, 1, t]], axis=0)
            xs = jnp.concatenate(split(x * scale_of(j)), axis=0)
            both = jnp.concatenate(split(tiles[idx[j, 0]]), axis=0)
            y = lax.dot_general(xs, both, (((1,), (1,)), ((), ())), preferred_element_type=F32)
            y = y[:width] + y[width:]
            prods[j] = y[:, :TL] + y[:, TL:]

    def gram_of(parts):
        acc = jnp.zeros((2 * width, 2 * width), F32)
        for x in parts:
            xx = jnp.concatenate(split(x), axis=0)
            acc = acc + lax.dot_general(
                xx, xx, (((1,), (1,)), ((), ())), preferred_element_type=F32
            )
        return pack(fold(acc))

    def own_tile(t):
        return jnp.concatenate([pt[t // tps, z, gi, h, t % tps] for h in range(2)], axis=0)

    def arrive(st, k):
        zs = (z + nz - k) % nz
        i = st * nz + k
        if k:
            remote(
                pt.at[st, zs, gi], pt.at[st, zs, gi], az_send.at[st, 0], az_recv.at[st, zs], to_z(zs)
            ).wait_recv()
        spread(st, k + 1)
        ag(pt.at[st, zs, gi, 0], i, 0, to_y)
        ag(pt.at[st, zs, gi, 1], i, 1, to_x)
        ag(pt.at[st, zs, gi, 0], i, 2, to_x)
        ag(pt.at[st, zs, gi, 1], i, 3, to_y)
        right_tiles(st, zs, gi)

    def relay(st, k):
        zs = (z + nz - k) % nz
        i = st * nz + k
        ag_wait(pt.at[st, zs, gy, 0], i, 0)
        ag(pt.at[st, zs, gy, 0], i, 4, to_x)
        ag_wait(pt.at[st, zs, gx, 1], i, 1)
        ag(pt.at[st, zs, gx, 1], i, 5, to_y)

    def finish(st, k):
        zs = (z + nz - k) % nz
        i = st * nz + k
        ag_wait(pt.at[st, zs, gx, 0], i, 2)
        right_tiles(st, zs, gx)
        ag_wait(pt.at[st, zs, gy, 1], i, 3)
        right_tiles(st, zs, gy)
        ag_wait(pt.at[st, zs, gd, 0], i, 4)
        ag_wait(pt.at[st, zs, gd, 1], i, 5)
        right_tiles(st, zs, gd)

    def sum_start(buf, mine, n, x, ssem, rsem, to):
        buf[mine] = x
        for k in range(1, n):
            send(buf.at[mine], buf.at[mine], ssem.at[k - 1], rsem.at[mine], to((mine + k) % n))

    def sum_end(buf, mine, n, ssem, rsem, to):
        for k in range(1, n):
            o = (mine + k) % n
            remote(buf.at[o], buf.at[o], ssem.at[k - 1], rsem.at[o], to(o)).wait_recv()
        y = buf[0]
        for o in range(1, n):
            y = y + buf[o]
        return y

    def to_q(q):
        return {"row": base + q}

    first = (
        (g1c, mc, nc, c1_send, c1_recv, to_c),
        (g1q, gi, QUADS, q1_send, q1_recv, to_q),
        (g1z, z, nz, z1_send, z1_recv, to_z),
    )
    second = (
        (g2c, mc, nc, c2_send, c2_recv, to_c),
        (g2q, gi, QUADS, q2_send, q2_recv, to_q),
        (g2z, z, nz, z2_send, z2_recv, to_z),
    )

    def start(stage, x):
        buf, mine, n, ssem, rsem, to = stage
        sum_start(buf, mine, n, x, ssem, rsem, to)

    def end(stage):
        buf, mine, n, ssem, rsem, to = stage
        return sum_end(buf, mine, n, ssem, rsem, to)

    def first_factor(elim):
        elim.steps(width // 2, width)
        pair = elim.pair()
        pair_ref[...] = pair
        vf_out[...] = transpose_left(pair)
        for t in range(tp):
            x = jnp.concatenate([jnp.zeros((width, TL), F32), own_tile(t)], axis=0)
            v_out[:, t * TL : (t + 1) * TL] = jnp.dot(
                pair, x, precision=HIGH, preferred_element_type=F32
            )

    items = [(st, k) for st in range(ns) for k in range(nz)]
    ends = [(st + 1) * nz + (1 if st == ns - 1 else 2) for st in range(ns)]
    last = ends[-1]
    third, fourth = last + max(3, nz - 1), last + max(4, nz)
    for slot in range(last + nz + 2):
        if slot < len(items):
            compute(*items[slot])
        if slot == 0:
            own_term()
        if 0 <= slot - 1 < len(items):
            step2(*items[slot - 1])
        if 0 <= slot - 2 < len(items):
            step3(*items[slot - 2])
        for st, begin in enumerate(ends):
            if slot == begin:
                final(st)
            if 0 <= slot - begin < nz:
                arrive(st, slot - begin)
        for st, begin in enumerate(ends):
            if 0 <= slot - begin - 1 < nz:
                relay(st, slot - begin - 1)
        if slot == fourth:
            first_factor(elim)
        for st, begin in enumerate(ends):
            if 0 <= slot - begin - 2 < nz:
                finish(st, slot - begin - 2)
        if slot == last:
            start(first[0], gram_of(own_tile(t) for t in range(tp)))
        elif slot == last + 1:
            start(first[1], end(first[0]))
        elif slot == last + 2:
            start(first[2], end(first[1]))
        elif slot == third:
            elim = Elimination(unpack(end(first[2]) * (1.0 / total_cols)))
            elim.steps(0, width // 2)

    def row_terms(r, _):
        x = prods[idx[r * each, 2]]
        for i in range(1, each):
            x = x + prods[idx[r * each + i, 2]]
        terms[r] = x
        return 0

    for k in range(1, nc):
        cc = (mc + k) % nc
        lax.fori_loop(cc * rtc, cc * rtc + rtc, row_terms, 0)
        send(terms.at[pl.ds(cc * rtc, rtc)], got_terms.at[mc], t_send.at[k - 1], t_recv.at[mc], to_c(cc))
    lax.fori_loop(mc * rtc, mc * rtc + rtc, row_terms, 0)
    for k in range(1, nc):
        cc = (mc + k) % nc
        remote(got_terms.at[cc], got_terms.at[cc], t_send.at[k - 1], t_recv.at[cc], to_c(cc)).wait_recv()
    root = math.sqrt(total_rows / total_cols)

    pair = pair_ref[...]
    for i in range(rtc):
        r = mc * rtc + i
        x = terms[r]
        for k in range(1, nc):
            x = x + got_terms[(mc + k) % nc, i]
        uu = u[:, pl.ds(pl.multiple_of(r * TL, TL), TL)]
        qt[i] = jnp.dot(
            pair, jnp.concatenate([-uu, root * x], axis=0), precision=HIGH, preferred_element_type=F32
        )
    x = gram_of(qt[i] for i in range(rtc))
    for stage in second:
        start(stage, x)
        x = end(stage)
    pair2 = factor_pair(unpack(x * (1.0 / total_rows)))
    uf_out[...] = transpose_left(pair2)
    for i in range(rtc):
        y = jnp.concatenate([jnp.zeros((width, TL), F32), qt[i]], axis=0)
        u_out[:, i * TL : (i + 1) * TL] = jnp.dot(
            pair2, y, precision=HIGH, preferred_element_type=F32
        )
    for c in pending:
        c.wait_send()


def hand_out(*refs):
    for src, dst in zip(refs[:4], refs[4:]):
        dst[...] = src[...]


def per_device(tiles, tile_rows, tile_cols, exponents, u_basis, v_basis, prior):
    nr, nc = lax.axis_size("row"), lax.axis_size("col")
    nz = nr // QUADS
    local = tiles[0, 0]
    rows, cols = tile_rows[0], tile_cols[0]
    count = local.shape[0]
    width, block_rows = u_basis.shape
    block_cols = exponents.shape[0]
    rt, ct = block_rows // TL, block_cols // TL
    tp = ct // nr
    ns = 2 if tp % 2 == 0 else 1
    tps = tp // ns
    rtc = rt // nc
    half = width // 2
    expo = exponents.reshape(ct, 1, TL)
    dma = pltpu.SemaphoreType.DMA
    vm = pl.BlockSpec(memory_space=pltpu.VMEM)

    def sems(*shape):
        return [dma(shape), dma(shape)]

    outs = pl.pallas_call(
        functools.partial(kernel, nr, nc, block_rows * nr, block_cols * nc),
        out_shape=(
            jax.ShapeDtypeStruct((width, block_rows // nc), F32),
            jax.ShapeDtypeStruct((width, block_cols // nr), F32),
            jax.ShapeDtypeStruct((width, width), F32),
            jax.ShapeDtypeStruct((width, width), F32),
        ),
        in_specs=[pl.BlockSpec(memory_space=pl.ANY)] * 7,
        out_specs=(vm,) * 4,
        scratch_shapes=[
            pltpu.VMEM((1, count), jnp.int32),
            pltpu.VMEM((1, count), jnp.int32),
            pltpu.VMEM((count, TL, TL), F32),
            pltpu.VMEM((width, block_rows), F32),
            pltpu.VMEM((ct, 1, TL), jnp.int32),
            pltpu.VMEM((width, tp * TL), F32),
            pltpu.VMEM((width, width), F32),
            pltpu.VMEM((count, TL), jnp.int32),
            pltpu.SMEM((count, TL), jnp.int32),
            dma((8,)),
            pltpu.VMEM((rt, 2 * width, TL), BF16),
            pltpu.VMEM((ns, nz, QUADS, 2, tps, half, TL), F32),
            pltpu.VMEM((ns * nz, 6, tps, half, TL), F32),
            pltpu.VMEM((ns, nz, 2, tps, half, TL), F32),
            pltpu.VMEM((width, tp * TL), F32),
            pltpu.VMEM((ns, nz, QUADS, 2, tps, half, TL), F32),
            pltpu.VMEM((ct, width, TL), F32),
            pltpu.VMEM((rt, width, TL), F32),
            pltpu.VMEM((nc, rtc, width, TL), F32),
            *[pltpu.VMEM((n, half, 2 * width), F32) for n in (nc, QUADS, nz)] * 2,
            pltpu.VMEM((rtc, width, TL), F32),
            pltpu.VMEM((width, 2 * width), F32),
            *sems(ns * nz, 6),
            *sems(ns, nz),
            *sems(ns, nz),
            *sems(ns * nz, 6),
            *sems(nc),
            *[x for n in (nc, QUADS, nz) for x in sems(n)] * 2,
        ],
        compiler_params=pltpu.CompilerParams(
            collective_id=0, has_side_effects=True, vmem_limit_bytes=56 * 1024 * 1024
        ),
    )(rows, cols, local, u_basis, expo, v_basis, prior)
    return pl.pallas_call(
        hand_out,
        out_shape=tuple(jax.ShapeDtypeStruct(o.shape, o.dtype) for o in outs),
        in_specs=[vm] * 4,
        out_specs=(vm,) * 4,
    )(*outs)


def solution(mesh):
    placed = (
        P("row", "col", None, None, None),
        P("row", "col", None),
        P("row", "col", None),
        P("col"),
        P(None, "row"),
        P(None, ("col", "row")),
        P(),
    )
    return jax.shard_map(
        per_device,
        mesh=mesh,
        in_specs=placed,
        out_specs=(P(None, ("row", "col")), P(None, ("col", "row")), P(), P()),
        check_vma=False,
    )
```

```python
import functools
import math

import jax
import jax.numpy as jnp
from jax import lax
from jax.experimental import pallas as pl
from jax.experimental.pallas import tpu as pltpu
from jax.sharding import PartitionSpec as P

F32 = jnp.float32
BF16 = jnp.bfloat16
HIGH = lax.Precision.HIGHEST
TL = 128
QUADS = 4


def split(x):
    hi = x.astype(BF16)
    return hi, (x - hi.astype(F32)).astype(BF16)


def fold(x):
    w = x.shape[0] // 2
    y = x[:w] + x[w:]
    return y + pltpu.roll(y, w, 1)


def stacked(x):
    return jnp.concatenate(split(x), axis=0)


def times(left, x):
    w = left.shape[0] // 2
    y = jnp.dot(left, jnp.concatenate(split(x), axis=1), preferred_element_type=F32)
    y = y[:w] + y[w:]
    return y[:, :TL] + y[:, TL:]


def pack(x):
    w = x.shape[0]
    lane = lax.broadcasted_iota(jnp.int32, (w // 2, 2 * w), 1)
    return jnp.where(lane < w, x[: w // 2], x[w // 2 :])


def unpack(x):
    w = x.shape[1] // 2
    lane = lax.broadcasted_iota(jnp.int32, x.shape, 1)
    y = pltpu.roll(x, w, 1)
    return jnp.concatenate([jnp.where(lane < w, x, y), jnp.where(lane < w, y, x)], axis=0)


class Elimination:
    def __init__(self, gram2):
        w = gram2.shape[0]
        self.row = lax.broadcasted_iota(jnp.int32, (w, 2 * w), 0)
        self.lane = lax.broadcasted_iota(jnp.int32, (w, 2 * w), 1)
        unit = jnp.where(self.lane - w == self.row, 1.0, 0.0).astype(F32)
        self.m = jnp.where(self.lane < w, gram2, unit)
        self.done, self.top, self.width = [], 0, w

    def steps(self, begin, end, block=4):
        m, top = self.m, self.top
        for j in range(begin, end, block):
            o = j - top
            below = self.row[top:]
            cols = [jnp.broadcast_to(m[:, j + i : j + i + 1], m.shape) for i in range(block)]
            rows = [m[o + i : o + i + 1] for i in range(block)]
            a = {(i, l): cols[l][o + i : o + i + 1] for i in range(block) for l in range(i, block)}
            for i in range(block):
                inv = 1.0 / a[i, i]
                m = m - jnp.where(below > j + i, cols[i], 0.0) * (rows[i] * inv)
                for l in range(i + 1, block):
                    s = a[i, l] * inv
                    rows[l] = rows[l] - s * rows[i]
                    cols[l] = cols[l] - s * cols[i]
                    for q in range(l, block):
                        a[l, q] = a[l, q] - s * a[i, q]
            if (j + block) % 8 == 0:
                self.done.append(m[:8])
                m = m[8:]
                top += 8
        self.m, self.top = m, top

    def pair(self):
        row, lane, w = self.row, self.lane, self.width
        m = jnp.concatenate(self.done, axis=0)
        diag = jnp.sum(jnp.where(lane == row, m, 0.0), axis=1, keepdims=True)
        m = m * (1.0 / jnp.sqrt(diag))
        return jnp.where((lane >= w) | (lane >= row), m, 0.0)


def factor_pair(gram2):
    e = Elimination(gram2)
    e.steps(0, gram2.shape[0])
    return e.pair()


def transpose_left(pair):
    w = pair.shape[0]
    return jnp.concatenate([pair, pair], axis=0).T[:w, :w]


def tile_lists(rows_in, cols_in, lists, row_count, col_count):
    n = rows_in.shape[1]
    rows = jnp.broadcast_to(rows_in[...], (n, n))
    cols = jnp.broadcast_to(cols_in[...], (n, n))
    down = lax.broadcasted_iota(jnp.int32, (n, n), 0)
    across = lax.broadcasted_iota(jnp.int32, (n, n), 1)
    key = rows * n + across
    key_down = jnp.sum(jnp.where(down == across, key, 0), axis=1, keepdims=True)
    rank = jnp.sum(jnp.where(key_down < key, 1, 0), axis=0, keepdims=True)
    hit = cols == down
    tile = jnp.max(jnp.where(hit, across, 0), axis=1, keepdims=True)
    tile_row = jnp.clip(jnp.max(jnp.where(hit, rows, 0), axis=1, keepdims=True), 0, row_count - 1)
    ordered = jnp.clip(
        jnp.max(jnp.where(rank == down, cols, 0), axis=1, keepdims=True), 0, col_count - 1
    )
    lane = lax.broadcasted_iota(jnp.int32, lists.shape, 1)
    lists[...] = jnp.where(lane == 0, tile, jnp.where(lane == 1, tile_row, ordered))


def kernel(
    nr, nc, total_rows, total_cols,
    rows_hbm, cols_hbm, tiles_hbm, u_hbm, expo_hbm, v_hbm, prior_hbm,
    u_out, v_out, vf_out, uf_out,
    rows_in, cols_in, tiles, u, expo, v, prior, lists, idx, in_sem,
    u2, part, got, gotz, own, pt, prods, terms, got_terms, g1c, g1q, g1z, g2c, g2q, g2z, qt, pair_ref,
    rs_send, rs_recv, z_send, z_recv, az_send, az_recv, ag_send, ag_recv,
    t_send, t_recv, c1_send, c1_recv, q1_send, q1_recv, z1_send, z1_recv,
    c2_send, c2_recv, q2_send, q2_recv, z2_send, z2_recv,
):
    nz = nr // QUADS
    width = u.shape[0]
    half = width // 2
    rt = terms.shape[0]
    rtc = rt // nc
    ns, tps = part.shape[0], part.shape[4]
    tp = ns * tps
    each = tiles.shape[0] // rt
    me = lax.axis_index("row")
    mc = lax.axis_index("col")
    z = me // QUADS
    gi = me % QUADS
    gx = gi + 1 - 2 * (gi % 2)
    gy = gi + 2 - 4 * (gi // 2)
    gd = (QUADS - 1) - gi
    base = z * QUADS
    to_x = {"row": base + gx}
    to_y = {"row": base + gy}
    to_d = {"row": base + gd}

    def to_z(zz):
        return {"row": zz * QUADS + gi}

    def to_c(cc):
        return {"col": cc}

    pending = []

    def remote(src, dst, ssem, rsem, dev):
        return pltpu.make_async_remote_copy(
            src_ref=src, dst_ref=dst, send_sem=ssem, recv_sem=rsem, device_id=dev,
            device_id_type=pl.DeviceIdType.MESH,
        )

    def send(*a):
        c = remote(*a)
        c.start()
        pending.append(c)

    quarter = tiles.shape[0] // 4
    fetch = [
        pltpu.make_async_copy(src, dst, in_sem.at[i])
        for i, (src, dst) in enumerate((
            (rows_hbm, rows_in), (cols_hbm, cols_in), (u_hbm, u),
            *[
                (tiles_hbm.at[i : i + quarter], tiles.at[i : i + quarter])
                for i in range(0, tiles.shape[0], quarter)
            ],
            (expo_hbm, expo), (v_hbm, v), (prior_hbm, prior),
        ))
    ]
    for c in fetch:
        c.start()
    barrier = pltpu.get_barrier_semaphore()
    peers = [to_x, to_y, to_d]
    peers += [to_z((z + k) % nz) for k in range(1, nz)]
    peers += [to_c((mc + k) % nc) for k in range(1, nc)]
    for p in peers:
        pl.semaphore_signal(barrier, inc=1, device_id=p, device_id_type=pl.DeviceIdType.MESH)

    for c in fetch[:2]:
        c.wait()
    tile_lists(rows_in, cols_in, lists, rt, expo.shape[0])
    to_scalars = pltpu.make_async_copy(lists, idx, in_sem.at[len(fetch)])
    to_scalars.start()
    fetch[2].wait()
    for r in range(rt):
        hi, lo = split(u[:, r * TL : (r + 1) * TL])
        u2[r, 0:width] = hi
        u2[r, width : 2 * width] = lo

    to_scalars.wait()
    for c in fetch[3:]:
        c.wait()

    def left_tile(j):
        th, tl_ = split(tiles[idx[j, 0]])
        both = jnp.concatenate([th, tl_], axis=1)
        x = jnp.dot(u2[idx[j, 1]], both, preferred_element_type=F32)
        y = x[:width] + x[width:]
        return y[:, :TL] + y[:, TL:]

    def column(st, zz, q, t):
        return (zz * QUADS + q) * tp + st * tps + t

    def compute(st, k):
        zz = (z + 1 + k) % nz
        i = st * nz + k
        for n, q in enumerate((gd, gx, gy, gi)):
            for t in range(tps):
                y = left_tile(column(st, zz, q, t))
                part[st, zz, q, 0, t] = y[:half]
                part[st, zz, q, 1, t] = y[half:]
            if n == 0 and i == 0:
                pl.semaphore_wait(barrier, len(peers))
            if n == 0:
                rs(part.at[st, zz, q, 0], i, 0, to_x)
                rs(part.at[st, zz, q, 1], i, 1, to_y)
            elif n == 1:
                rs(part.at[st, zz, q, 0], i, 2, to_x)
            elif n == 2:
                rs(part.at[st, zz, q, 1], i, 3, to_y)

    def rs(src, i, n, dev):
        send(src, got.at[i, n], rs_send.at[i, n], rs_recv.at[i, n], dev)

    def rs_wait(i, n):
        remote(got.at[i, n], got.at[i, n], rs_send.at[i, n], rs_recv.at[i, n], to_x).wait_recv()

    def step2(st, k):
        zz = (z + 1 + k) % nz
        i = st * nz + k
        rs_wait(i, 0)
        part[st, zz, gy, 0] = part[st, zz, gy, 0] + got[i, 0]
        rs(part.at[st, zz, gy, 0], i, 4, to_y)
        rs_wait(i, 1)
        part[st, zz, gx, 1] = part[st, zz, gx, 1] + got[i, 1]
        rs(part.at[st, zz, gx, 1], i, 5, to_x)

    def step3(st, k):
        zz = (z + 1 + k) % nz
        i = st * nz + k
        for n in (2, 3, 4, 5):
            rs_wait(i, n)
        part[st, zz, gi, 0] = part[st, zz, gi, 0] + (got[i, 2] + got[i, 4])
        part[st, zz, gi, 1] = part[st, zz, gi, 1] + (got[i, 3] + got[i, 5])
        if k < nz - 1:
            send(part.at[st, zz, gi], gotz.at[st, z], z_send.at[st, k], z_recv.at[st, z], to_z(zz))

    def own_term():
        tri = lax.broadcasted_iota(jnp.int32, prior.shape, 0) >= lax.broadcasted_iota(
            jnp.int32, prior.shape, 1
        )
        low = jnp.where(tri, prior[...], 0.0)
        own[...] = jnp.dot(low, v[...], precision=HIGH, preferred_element_type=F32)

    def scale_of(j):
        e = expo[j]
        return jnp.where((e & 1) == 1, 0.5, 1.0) * jnp.where(e >= 2, 0.25, 1.0)

    def final(st):
        for k in range(1, nz):
            zs = (z + k) % nz
            remote(
                gotz.at[st, zs], gotz.at[st, zs], z_send.at[st, k - 1], z_recv.at[st, zs], to_z(zs)
            ).wait_recv()
        for t in range(tps):
            at = (st * tps + t) * TL
            sc = scale_of(column(st, z, gi, t))
            for h in range(2):
                x = part[st, z, gi, h, t]
                for k in range(1, nz):
                    x = x + gotz[st, (z + k) % nz, h, t]
                pt[st, z, gi, h, t] = x * sc - own[h * half : (h + 1) * half, at : at + TL]

    def spread(st, k):
        if 1 <= k < nz:
            zs = (z + k) % nz
            send(
                pt.at[st, z, gi], pt.at[st, z, gi], az_send.at[st, k - 1], az_recv.at[st, z], to_z(zs)
            )

    def ag(src, k, n, dev):
        send(src, src, ag_send.at[k, n], ag_recv.at[k, n], dev)

    def ag_wait(dst, k, n):
        remote(dst, dst, ag_send.at[k, n], ag_recv.at[k, n], to_x).wait_recv()

    def right_tiles(st, zz, q):
        for t in range(tps):
            j = column(st, zz, q, t)
            x = jnp.concatenate([pt[st, zz, q, 0, t], pt[st, zz, q, 1, t]], axis=0)
            xs = jnp.concatenate(split(x * scale_of(j)), axis=0)
            both = jnp.concatenate(split(tiles[idx[j, 0]]), axis=0)
            y = lax.dot_general(xs, both, (((1,), (1,)), ((), ())), preferred_element_type=F32)
            y = y[:width] + y[width:]
            prods[j] = y[:, :TL] + y[:, TL:]

    def gram_of(parts):
        acc = jnp.zeros((2 * width, 2 * width), F32)
        for x in parts:
            xx = jnp.concatenate(split(x), axis=0)
            acc = acc + lax.dot_general(
                xx, xx, (((1,), (1,)), ((), ())), preferred_element_type=F32
            )
        return pack(fold(acc))

    def own_tile(t):
        return jnp.concatenate([pt[t // tps, z, gi, h, t % tps] for h in range(2)], axis=0)

    def arrive(st, k):
        zs = (z + nz - k) % nz
        i = st * nz + k
        if k:
            remote(
                pt.at[st, zs, gi], pt.at[st, zs, gi], az_send.at[st, 0], az_recv.at[st, zs], to_z(zs)
            ).wait_recv()
        spread(st, k + 1)
        ag(pt.at[st, zs, gi, 0], i, 0, to_y)
        ag(pt.at[st, zs, gi, 1], i, 1, to_x)
        ag(pt.at[st, zs, gi, 0], i, 2, to_x)
        ag(pt.at[st, zs, gi, 1], i, 3, to_y)
        right_tiles(st, zs, gi)

    def relay(st, k):
        zs = (z + nz - k) % nz
        i = st * nz + k
        ag_wait(pt.at[st, zs, gy, 0], i, 0)
        ag(pt.at[st, zs, gy, 0], i, 4, to_x)
        ag_wait(pt.at[st, zs, gx, 1], i, 1)
        ag(pt.at[st, zs, gx, 1], i, 5, to_y)

    def finish(st, k):
        zs = (z + nz - k) % nz
        i = st * nz + k
        ag_wait(pt.at[st, zs, gx, 0], i, 2)
        right_tiles(st, zs, gx)
        ag_wait(pt.at[st, zs, gy, 1], i, 3)
        right_tiles(st, zs, gy)
        ag_wait(pt.at[st, zs, gd, 0], i, 4)
        ag_wait(pt.at[st, zs, gd, 1], i, 5)
        right_tiles(st, zs, gd)

    def sum_start(buf, mine, n, x, ssem, rsem, to):
        buf[mine] = x
        for k in range(1, n):
            send(buf.at[mine], buf.at[mine], ssem.at[k - 1], rsem.at[mine], to((mine + k) % n))

    def sum_end(buf, mine, n, ssem, rsem, to):
        for k in range(1, n):
            o = (mine + k) % n
            remote(buf.at[o], buf.at[o], ssem.at[k - 1], rsem.at[o], to(o)).wait_recv()
        y = buf[0]
        for o in range(1, n):
            y = y + buf[o]
        return y

    def to_q(q):
        return {"row": base + q}

    first = (
        (g1c, mc, nc, c1_send, c1_recv, to_c),
        (g1q, gi, QUADS, q1_send, q1_recv, to_q),
        (g1z, z, nz, z1_send, z1_recv, to_z),
    )
    second = (
        (g2c, mc, nc, c2_send, c2_recv, to_c),
        (g2q, gi, QUADS, q2_send, q2_recv, to_q),
        (g2z, z, nz, z2_send, z2_recv, to_z),
    )

    def start(stage, x):
        buf, mine, n, ssem, rsem, to = stage
        sum_start(buf, mine, n, x, ssem, rsem, to)

    def end(stage):
        buf, mine, n, ssem, rsem, to = stage
        return sum_end(buf, mine, n, ssem, rsem, to)

    def first_factor(elim):
        elim.steps(width // 2, width)
        pair = elim.pair()
        pair_ref[...] = pair
        vf_out[...] = transpose_left(pair)
        for t in range(tp):
            x = jnp.concatenate([jnp.zeros((width, TL), F32), own_tile(t)], axis=0)
            v_out[:, t * TL : (t + 1) * TL] = times(stacked(pair), x)

    items = [(st, k) for st in range(ns) for k in range(nz)]
    ends = [(st + 1) * nz + (1 if st == ns - 1 else 2) for st in range(ns)]
    last = ends[-1]
    third, fourth = last + max(3, nz - 1), last + max(4, nz)
    for slot in range(last + nz + 2):
        if slot < len(items):
            compute(*items[slot])
        if slot == 0:
            own_term()
        if 0 <= slot - 1 < len(items):
            step2(*items[slot - 1])
        if 0 <= slot - 2 < len(items):
            step3(*items[slot - 2])
        for st, begin in enumerate(ends):
            if slot == begin:
                final(st)
            if 0 <= slot - begin < nz:
                arrive(st, slot - begin)
        for st, begin in enumerate(ends):
            if 0 <= slot - begin - 1 < nz:
                relay(st, slot - begin - 1)
        if slot == fourth:
            first_factor(elim)
        for st, begin in enumerate(ends):
            if 0 <= slot - begin - 2 < nz:
                finish(st, slot - begin - 2)
        if slot == last:
            start(first[0], gram_of(own_tile(t) for t in range(tp)))
        elif slot == last + 1:
            start(first[1], end(first[0]))
        elif slot == last + 2:
            start(first[2], end(first[1]))
        elif slot == third:
            elim = Elimination(unpack(end(first[2]) * (1.0 / total_cols)))
            elim.steps(0, width // 2)

    def row_terms(r):
        x = prods[idx[r * each, 2]]
        for i in range(1, each):
            x = x + prods[idx[r * each + i, 2]]
        terms[r] = x

    for k in range(1, nc):
        cc = (mc + k) % nc
        for i in range(rtc):
            row_terms(cc * rtc + i)
        send(terms.at[pl.ds(cc * rtc, rtc)], got_terms.at[mc], t_send.at[k - 1], t_recv.at[mc], to_c(cc))
    for i in range(rtc):
        row_terms(mc * rtc + i)
    for k in range(1, nc):
        cc = (mc + k) % nc
        remote(got_terms.at[cc], got_terms.at[cc], t_send.at[k - 1], t_recv.at[cc], to_c(cc)).wait_recv()
    root = math.sqrt(total_rows / total_cols)

    left = stacked(pair_ref[...])
    for i in range(rtc):
        r = mc * rtc + i
        x = terms[r]
        for k in range(1, nc):
            x = x + got_terms[(mc + k) % nc, i]
        uu = u[:, pl.ds(pl.multiple_of(r * TL, TL), TL)]
        qt[i] = times(left, jnp.concatenate([-uu, root * x], axis=0))
    x = gram_of(qt[i] for i in range(rtc))
    for stage in second:
        start(stage, x)
        x = end(stage)
    pair2 = factor_pair(unpack(x * (1.0 / total_rows)))
    left2 = stacked(pair2)
    uf_out[...] = transpose_left(pair2)
    for i in range(rtc):
        y = jnp.concatenate([jnp.zeros((width, TL), F32), qt[i]], axis=0)
        u_out[:, i * TL : (i + 1) * TL] = times(left2, y)
    for c in pending:
        c.wait_send()


def hand_out(*refs):
    for src, dst in zip(refs[:4], refs[4:]):
        dst[...] = src[...]


def per_device(tiles, tile_rows, tile_cols, exponents, u_basis, v_basis, prior):
    nr, nc = lax.axis_size("row"), lax.axis_size("col")
    nz = nr // QUADS
    local = tiles[0, 0]
    rows, cols = tile_rows[0], tile_cols[0]
    count = local.shape[0]
    width, block_rows = u_basis.shape
    block_cols = exponents.shape[0]
    rt, ct = block_rows // TL, block_cols // TL
    tp = ct // nr
    ns = 1
    tps = tp // ns
    rtc = rt // nc
    half = width // 2
    expo = exponents.reshape(ct, 1, TL)
    dma = pltpu.SemaphoreType.DMA
    vm = pl.BlockSpec(memory_space=pltpu.VMEM)

    def sems(*shape):
        return [dma(shape), dma(shape)]

    outs = pl.pallas_call(
        functools.partial(kernel, nr, nc, block_rows * nr, block_cols * nc),
        out_shape=(
            jax.ShapeDtypeStruct((width, block_rows // nc), F32),
            jax.ShapeDtypeStruct((width, block_cols // nr), F32),
            jax.ShapeDtypeStruct((width, width), F32),
            jax.ShapeDtypeStruct((width, width), F32),
        ),
        in_specs=[pl.BlockSpec(memory_space=pl.ANY)] * 7,
        out_specs=(vm,) * 4,
        scratch_shapes=[
            pltpu.VMEM((1, count), jnp.int32),
            pltpu.VMEM((1, count), jnp.int32),
            pltpu.VMEM((count, TL, TL), F32),
            pltpu.VMEM((width, block_rows), F32),
            pltpu.VMEM((ct, 1, TL), jnp.int32),
            pltpu.VMEM((width, tp * TL), F32),
            pltpu.VMEM((width, width), F32),
            pltpu.VMEM((count, TL), jnp.int32),
            pltpu.SMEM((count, TL), jnp.int32),
            dma((11,)),
            pltpu.VMEM((rt, 2 * width, TL), BF16),
            pltpu.VMEM((ns, nz, QUADS, 2, tps, half, TL), F32),
            pltpu.VMEM((ns * nz, 6, tps, half, TL), F32),
            pltpu.VMEM((ns, nz, 2, tps, half, TL), F32),
            pltpu.VMEM((width, tp * TL), F32),
            pltpu.VMEM((ns, nz, QUADS, 2, tps, half, TL), F32),
            pltpu.VMEM((ct, width, TL), F32),
            pltpu.VMEM((rt, width, TL), F32),
            pltpu.VMEM((nc, rtc, width, TL), F32),
            *[pltpu.VMEM((n, half, 2 * width), F32) for n in (nc, QUADS, nz)] * 2,
            pltpu.VMEM((rtc, width, TL), F32),
            pltpu.VMEM((width, 2 * width), F32),
            *sems(ns * nz, 6),
            *sems(ns, nz),
            *sems(ns, nz),
            *sems(ns * nz, 6),
            *sems(nc),
            *[x for n in (nc, QUADS, nz) for x in sems(n)] * 2,
        ],
        compiler_params=pltpu.CompilerParams(
            collective_id=0, has_side_effects=True, vmem_limit_bytes=56 * 1024 * 1024
        ),
    )(rows, cols, local, u_basis, expo, v_basis, prior)
    return pl.pallas_call(
        hand_out,
        out_shape=tuple(jax.ShapeDtypeStruct(o.shape, o.dtype) for o in outs),
        in_specs=[vm] * 4,
        out_specs=(vm,) * 4,
    )(*outs)


def solution(mesh):
    placed = (
        P("row", "col", None, None, None),
        P("row", "col", None),
        P("row", "col", None),
        P("col"),
        P(None, "row"),
        P(None, ("col", "row")),
        P(),
    )
    return jax.shard_map(
        per_device,
        mesh=mesh,
        in_specs=placed,
        out_specs=(P(None, ("row", "col")), P(None, ("col", "row")), P(), P()),
        check_vma=False,
    )
```

```python
import functools
import math

import jax
import jax.numpy as jnp
from jax import lax
from jax.experimental import pallas as pl
from jax.experimental.pallas import tpu as pltpu
from jax.sharding import PartitionSpec as P

F32 = jnp.float32
BF16 = jnp.bfloat16
HIGH = lax.Precision.HIGHEST
TL = 128
QUADS = 4


def split(x):
    hi = x.astype(BF16)
    return hi, (x - hi.astype(F32)).astype(BF16)


def fold(x):
    w = x.shape[0] // 2
    y = x[:w] + x[w:]
    return y + pltpu.roll(y, w, 1)


def stacked(x):
    return jnp.concatenate(split(x), axis=0)


def times(left, x):
    w = left.shape[0] // 2
    y = jnp.dot(left, jnp.concatenate(split(x), axis=1), preferred_element_type=F32)
    y = y[:w] + y[w:]
    return y[:, :TL] + y[:, TL:]


def pack(x):
    w = x.shape[0]
    lane = lax.broadcasted_iota(jnp.int32, (w // 2, 2 * w), 1)
    return jnp.where(lane < w, x[: w // 2], x[w // 2 :])


def unpack(x):
    w = x.shape[1] // 2
    lane = lax.broadcasted_iota(jnp.int32, x.shape, 1)
    y = pltpu.roll(x, w, 1)
    return jnp.concatenate([jnp.where(lane < w, x, y), jnp.where(lane < w, y, x)], axis=0)


class Elimination:
    def __init__(self, gram2):
        w = gram2.shape[0]
        self.row = lax.broadcasted_iota(jnp.int32, (w, 2 * w), 0)
        self.lane = lax.broadcasted_iota(jnp.int32, (w, 2 * w), 1)
        unit = jnp.where(self.lane - w == self.row, 1.0, 0.0).astype(F32)
        self.m = jnp.where(self.lane < w, gram2, unit)
        self.done, self.top, self.width = [], 0, w

    def steps(self, begin, end, block=4):
        m, top = self.m, self.top
        for j in range(begin, end, block):
            o = j - top
            below = self.row[top:]
            cols = [jnp.broadcast_to(m[:, j + i : j + i + 1], m.shape) for i in range(block)]
            rows = [m[o + i : o + i + 1] for i in range(block)]
            a = {(i, l): cols[l][o + i : o + i + 1] for i in range(block) for l in range(i, block)}
            for i in range(block):
                inv = 1.0 / a[i, i]
                m = m - jnp.where(below > j + i, cols[i], 0.0) * (rows[i] * inv)
                for l in range(i + 1, block):
                    s = a[i, l] * inv
                    rows[l] = rows[l] - s * rows[i]
                    cols[l] = cols[l] - s * cols[i]
                    for q in range(l, block):
                        a[l, q] = a[l, q] - s * a[i, q]
            if (j + block) % 8 == 0:
                self.done.append(m[:8])
                m = m[8:]
                top += 8
        self.m, self.top = m, top

    def pair(self):
        row, lane, w = self.row, self.lane, self.width
        m = jnp.concatenate(self.done, axis=0)
        diag = jnp.sum(jnp.where(lane == row, m, 0.0), axis=1, keepdims=True)
        m = m * (1.0 / jnp.sqrt(diag))
        return jnp.where((lane >= w) | (lane >= row), m, 0.0)


def factor_pair(gram2):
    e = Elimination(gram2)
    e.steps(0, gram2.shape[0])
    return e.pair()


def transpose_left(pair):
    w = pair.shape[0]
    return jnp.concatenate([pair, pair], axis=0).T[:w, :w]


def tile_lists(rows_in, cols_in, lists, row_count, col_count):
    n = rows_in.shape[1]
    rows = jnp.broadcast_to(rows_in[...], (n, n))
    cols = jnp.broadcast_to(cols_in[...], (n, n))
    down = lax.broadcasted_iota(jnp.int32, (n, n), 0)
    across = lax.broadcasted_iota(jnp.int32, (n, n), 1)
    key = rows * n + across
    key_down = jnp.sum(jnp.where(down == across, key, 0), axis=1, keepdims=True)
    rank = jnp.sum(jnp.where(key_down < key, 1, 0), axis=0, keepdims=True)
    hit = cols == down
    tile = jnp.max(jnp.where(hit, across, 0), axis=1, keepdims=True)
    tile_row = jnp.clip(jnp.max(jnp.where(hit, rows, 0), axis=1, keepdims=True), 0, row_count - 1)
    ordered = jnp.clip(
        jnp.max(jnp.where(rank == down, cols, 0), axis=1, keepdims=True), 0, col_count - 1
    )
    lane = lax.broadcasted_iota(jnp.int32, lists.shape, 1)
    lists[...] = jnp.where(lane == 0, tile, jnp.where(lane == 1, tile_row, ordered))


def kernel(
    nr, nc, total_rows, total_cols,
    rows_hbm, cols_hbm, tiles_hbm, u_hbm, expo_hbm, v_hbm, prior_hbm,
    u_out, v_out, vf_out, uf_out,
    rows_in, cols_in, tiles, u, expo, v, prior, lists, idx, in_sem,
    u2, part, got, gotz, own, pt, prods, terms, got_terms, g1c, g1q, g1z, g2c, g2q, g2z, qt, pair_ref,
    rs_send, rs_recv, z_send, z_recv, az_send, az_recv, ag_send, ag_recv,
    t_send, t_recv, c1_send, c1_recv, q1_send, q1_recv, z1_send, z1_recv,
    c2_send, c2_recv, q2_send, q2_recv, z2_send, z2_recv,
):
    nz = nr // QUADS
    width = u.shape[0]
    half = width // 2
    rt = terms.shape[0]
    rtc = rt // nc
    ns, tps = part.shape[0], part.shape[4]
    tp = ns * tps
    each = tiles.shape[0] // rt
    me = lax.axis_index("row")
    mc = lax.axis_index("col")
    z = me // QUADS
    gi = me % QUADS
    gx = gi + 1 - 2 * (gi % 2)
    gy = gi + 2 - 4 * (gi // 2)
    gd = (QUADS - 1) - gi
    base = z * QUADS
    to_x = {"row": base + gx}
    to_y = {"row": base + gy}
    to_d = {"row": base + gd}

    near = sorted(range(nz), key=lambda o: min(o, nz - o))
    far = near[::-1]

    def to_z(zz):
        return {"row": zz * QUADS + gi}

    def to_c(cc):
        return {"col": cc}

    pending = []

    def remote(src, dst, ssem, rsem, dev):
        return pltpu.make_async_remote_copy(
            src_ref=src, dst_ref=dst, send_sem=ssem, recv_sem=rsem, device_id=dev,
            device_id_type=pl.DeviceIdType.MESH,
        )

    def send(*a):
        c = remote(*a)
        c.start()
        pending.append(c)

    quarter = tiles.shape[0] // 4
    fetch = [
        pltpu.make_async_copy(src, dst, in_sem.at[i])
        for i, (src, dst) in enumerate((
            (rows_hbm, rows_in), (cols_hbm, cols_in), (u_hbm, u),
            *[
                (tiles_hbm.at[i : i + quarter], tiles.at[i : i + quarter])
                for i in range(0, tiles.shape[0], quarter)
            ],
            (expo_hbm, expo), (v_hbm, v), (prior_hbm, prior),
        ))
    ]
    for c in fetch:
        c.start()
    barrier = pltpu.get_barrier_semaphore()
    peers = [to_x, to_y, to_d]
    peers += [to_z((z + k) % nz) for k in range(1, nz)]
    peers += [to_c((mc + k) % nc) for k in range(1, nc)]
    for p in peers:
        pl.semaphore_signal(barrier, inc=1, device_id=p, device_id_type=pl.DeviceIdType.MESH)

    for c in fetch[:2]:
        c.wait()
    tile_lists(rows_in, cols_in, lists, rt, expo.shape[0])
    to_scalars = pltpu.make_async_copy(lists, idx, in_sem.at[len(fetch)])
    to_scalars.start()
    fetch[2].wait()
    for r in range(rt):
        hi, lo = split(u[:, r * TL : (r + 1) * TL])
        u2[r, 0:width] = hi
        u2[r, width : 2 * width] = lo

    to_scalars.wait()
    for c in fetch[3:]:
        c.wait()

    def left_tile(j):
        th, tl_ = split(tiles[idx[j, 0]])
        both = jnp.concatenate([th, tl_], axis=1)
        x = jnp.dot(u2[idx[j, 1]], both, preferred_element_type=F32)
        y = x[:width] + x[width:]
        return y[:, :TL] + y[:, TL:]

    def column(st, zz, q, t):
        return (zz * QUADS + q) * tp + st * tps + t

    def compute(st, k):
        zz = (z + far[k]) % nz
        i = st * nz + k
        for n, q in enumerate((gd, gx, gy, gi)):
            for t in range(tps):
                y = left_tile(column(st, zz, q, t))
                part[st, zz, q, 0, t] = y[:half]
                part[st, zz, q, 1, t] = y[half:]
            if n == 0 and i == 0:
                pl.semaphore_wait(barrier, len(peers))
            if n == 0:
                rs(part.at[st, zz, q, 0], i, 0, to_x)
                rs(part.at[st, zz, q, 1], i, 1, to_y)
            elif n == 1:
                rs(part.at[st, zz, q, 0], i, 2, to_x)
            elif n == 2:
                rs(part.at[st, zz, q, 1], i, 3, to_y)

    def rs(src, i, n, dev):
        send(src, got.at[i, n], rs_send.at[i, n], rs_recv.at[i, n], dev)

    def rs_wait(i, n):
        remote(got.at[i, n], got.at[i, n], rs_send.at[i, n], rs_recv.at[i, n], to_x).wait_recv()

    def step2(st, k):
        zz = (z + far[k]) % nz
        i = st * nz + k
        rs_wait(i, 0)
        part[st, zz, gy, 0] = part[st, zz, gy, 0] + got[i, 0]
        rs(part.at[st, zz, gy, 0], i, 4, to_y)
        rs_wait(i, 1)
        part[st, zz, gx, 1] = part[st, zz, gx, 1] + got[i, 1]
        rs(part.at[st, zz, gx, 1], i, 5, to_x)

    def step3(st, k):
        zz = (z + far[k]) % nz
        i = st * nz + k
        for n in (2, 3, 4, 5):
            rs_wait(i, n)
        part[st, zz, gi, 0] = part[st, zz, gi, 0] + (got[i, 2] + got[i, 4])
        part[st, zz, gi, 1] = part[st, zz, gi, 1] + (got[i, 3] + got[i, 5])
        if k < nz - 1:
            send(part.at[st, zz, gi], gotz.at[st, z], z_send.at[st, k], z_recv.at[st, z], to_z(zz))

    def own_term():
        tri = lax.broadcasted_iota(jnp.int32, prior.shape, 0) >= lax.broadcasted_iota(
            jnp.int32, prior.shape, 1
        )
        low = jnp.where(tri, prior[...], 0.0)
        own[...] = jnp.dot(low, v[...], precision=HIGH, preferred_element_type=F32)

    def scale_of(j):
        e = expo[j]
        return jnp.where((e & 1) == 1, 0.5, 1.0) * jnp.where(e >= 2, 0.25, 1.0)

    def final(st):
        for k in range(1, nz):
            zs = (z + k) % nz
            remote(
                gotz.at[st, zs], gotz.at[st, zs], z_send.at[st, k - 1], z_recv.at[st, zs], to_z(zs)
            ).wait_recv()
        for t in range(tps):
            at = (st * tps + t) * TL
            sc = scale_of(column(st, z, gi, t))
            for h in range(2):
                x = part[st, z, gi, h, t]
                for k in range(1, nz):
                    x = x + gotz[st, (z + k) % nz, h, t]
                pt[st, z, gi, h, t] = x * sc - own[h * half : (h + 1) * half, at : at + TL]

    def spread(st, k):
        if 1 <= k < nz:
            zs = (z + near[k]) % nz
            send(
                pt.at[st, z, gi], pt.at[st, z, gi], az_send.at[st, k - 1], az_recv.at[st, z], to_z(zs)
            )

    def ag(src, k, n, dev):
        send(src, src, ag_send.at[k, n], ag_recv.at[k, n], dev)

    def ag_wait(dst, k, n):
        remote(dst, dst, ag_send.at[k, n], ag_recv.at[k, n], to_x).wait_recv()

    def right_tiles(st, zz, q):
        for t in range(tps):
            j = column(st, zz, q, t)
            x = jnp.concatenate([pt[st, zz, q, 0, t], pt[st, zz, q, 1, t]], axis=0)
            xs = jnp.concatenate(split(x * scale_of(j)), axis=0)
            both = jnp.concatenate(split(tiles[idx[j, 0]]), axis=0)
            y = lax.dot_general(xs, both, (((1,), (1,)), ((), ())), preferred_element_type=F32)
            y = y[:width] + y[width:]
            prods[j] = y[:, :TL] + y[:, TL:]

    def gram_of(parts):
        acc = jnp.zeros((2 * width, 2 * width), F32)
        for x in parts:
            xx = jnp.concatenate(split(x), axis=0)
            acc = acc + lax.dot_general(
                xx, xx, (((1,), (1,)), ((), ())), preferred_element_type=F32
            )
        return pack(fold(acc))

    def own_tile(t):
        return jnp.concatenate([pt[t // tps, z, gi, h, t % tps] for h in range(2)], axis=0)

    def arrive(st, k):
        zs = (z + nz - near[k]) % nz
        i = st * nz + k
        spread(st, k + 1)
        if k:
            remote(
                pt.at[st, zs, gi], pt.at[st, zs, gi], az_send.at[st, 0], az_recv.at[st, zs], to_z(zs)
            ).wait_recv()
        ag(pt.at[st, zs, gi, 0], i, 0, to_y)
        ag(pt.at[st, zs, gi, 1], i, 1, to_x)
        ag(pt.at[st, zs, gi, 0], i, 2, to_x)
        ag(pt.at[st, zs, gi, 1], i, 3, to_y)
        right_tiles(st, zs, gi)

    def relay(st, k):
        zs = (z + nz - near[k]) % nz
        i = st * nz + k
        ag_wait(pt.at[st, zs, gy, 0], i, 0)
        ag(pt.at[st, zs, gy, 0], i, 4, to_x)
        ag_wait(pt.at[st, zs, gx, 1], i, 1)
        ag(pt.at[st, zs, gx, 1], i, 5, to_y)

    def finish(st, k):
        zs = (z + nz - near[k]) % nz
        i = st * nz + k
        ag_wait(pt.at[st, zs, gx, 0], i, 2)
        right_tiles(st, zs, gx)
        ag_wait(pt.at[st, zs, gy, 1], i, 3)
        right_tiles(st, zs, gy)
        ag_wait(pt.at[st, zs, gd, 0], i, 4)
        ag_wait(pt.at[st, zs, gd, 1], i, 5)
        right_tiles(st, zs, gd)

    def sum_start(buf, mine, n, x, ssem, rsem, to):
        buf[mine] = x
        for k in range(1, n):
            send(buf.at[mine], buf.at[mine], ssem.at[k - 1], rsem.at[mine], to((mine + k) % n))

    def sum_end(buf, mine, n, ssem, rsem, to):
        for k in range(1, n):
            o = (mine + k) % n
            remote(buf.at[o], buf.at[o], ssem.at[k - 1], rsem.at[o], to(o)).wait_recv()
        y = buf[0]
        for o in range(1, n):
            y = y + buf[o]
        return y

    def to_q(q):
        return {"row": base + q}

    first = (
        (g1c, mc, nc, c1_send, c1_recv, to_c),
        (g1q, gi, QUADS, q1_send, q1_recv, to_q),
        (g1z, z, nz, z1_send, z1_recv, to_z),
    )
    second = (
        (g2c, mc, nc, c2_send, c2_recv, to_c),
        (g2q, gi, QUADS, q2_send, q2_recv, to_q),
        (g2z, z, nz, z2_send, z2_recv, to_z),
    )

    def start(stage, x):
        buf, mine, n, ssem, rsem, to = stage
        sum_start(buf, mine, n, x, ssem, rsem, to)

    def end(stage):
        buf, mine, n, ssem, rsem, to = stage
        return sum_end(buf, mine, n, ssem, rsem, to)

    def first_factor(elim):
        elim.steps(width // 2, width)
        pair = elim.pair()
        pair_ref[...] = pair
        vf_out[...] = transpose_left(pair)
        for t in range(tp):
            x = jnp.concatenate([jnp.zeros((width, TL), F32), own_tile(t)], axis=0)
            v_out[:, t * TL : (t + 1) * TL] = times(stacked(pair), x)

    items = [(st, k) for st in range(ns) for k in range(nz)]
    ends = [(st + 1) * nz + (1 if st == ns - 1 else 2) for st in range(ns)]
    last = ends[-1]
    third, fourth = last + max(3, nz - 1), last + max(4, nz)
    for slot in range(last + nz + 2):
        if slot < len(items):
            compute(*items[slot])
        if slot == 0:
            own_term()
        if 0 <= slot - 1 < len(items):
            step2(*items[slot - 1])
        if 0 <= slot - 2 < len(items):
            step3(*items[slot - 2])
        for st, begin in enumerate(ends):
            if 0 <= slot - begin - 1 < nz:
                relay(st, slot - begin - 1)
        for st, begin in enumerate(ends):
            if slot == begin:
                final(st)
            if 0 <= slot - begin < nz:
                arrive(st, slot - begin)
        if slot == fourth:
            first_factor(elim)
        for st, begin in enumerate(ends):
            if 0 <= slot - begin - 2 < nz:
                finish(st, slot - begin - 2)
        if slot == last:
            start(first[0], gram_of(own_tile(t) for t in range(tp)))
        elif slot == last + 1:
            start(first[1], end(first[0]))
        elif slot == last + 2:
            start(first[2], end(first[1]))
        elif slot == third:
            elim = Elimination(unpack(end(first[2]) * (1.0 / total_cols)))
            elim.steps(0, width // 2)

    def row_terms(r):
        x = prods[idx[r * each, 2]]
        for i in range(1, each):
            x = x + prods[idx[r * each + i, 2]]
        terms[r] = x

    for k in range(1, nc):
        cc = (mc + k) % nc
        for i in range(rtc):
            row_terms(cc * rtc + i)
        send(terms.at[pl.ds(cc * rtc, rtc)], got_terms.at[mc], t_send.at[k - 1], t_recv.at[mc], to_c(cc))
    for i in range(rtc):
        row_terms(mc * rtc + i)
    for k in range(1, nc):
        cc = (mc + k) % nc
        remote(got_terms.at[cc], got_terms.at[cc], t_send.at[k - 1], t_recv.at[cc], to_c(cc)).wait_recv()
    root = math.sqrt(total_rows / total_cols)

    left = stacked(pair_ref[...])
    for i in range(rtc):
        r = mc * rtc + i
        x = terms[r]
        for k in range(1, nc):
            x = x + got_terms[(mc + k) % nc, i]
        uu = u[:, pl.ds(pl.multiple_of(r * TL, TL), TL)]
        qt[i] = times(left, jnp.concatenate([-uu, root * x], axis=0))
    x = gram_of(qt[i] for i in range(rtc))
    for stage in second:
        start(stage, x)
        x = end(stage)
    pair2 = factor_pair(unpack(x * (1.0 / total_rows)))
    left2 = stacked(pair2)
    uf_out[...] = transpose_left(pair2)
    for i in range(rtc):
        y = jnp.concatenate([jnp.zeros((width, TL), F32), qt[i]], axis=0)
        u_out[:, i * TL : (i + 1) * TL] = times(left2, y)
    for c in pending:
        c.wait_send()


def hand_out(*refs):
    for src, dst in zip(refs[:4], refs[4:]):
        dst[...] = src[...]


def per_device(tiles, tile_rows, tile_cols, exponents, u_basis, v_basis, prior):
    nr, nc = lax.axis_size("row"), lax.axis_size("col")
    nz = nr // QUADS
    local = tiles[0, 0]
    rows, cols = tile_rows[0], tile_cols[0]
    count = local.shape[0]
    width, block_rows = u_basis.shape
    block_cols = exponents.shape[0]
    rt, ct = block_rows // TL, block_cols // TL
    tp = ct // nr
    ns = 1
    tps = tp // ns
    rtc = rt // nc
    half = width // 2
    expo = exponents.reshape(ct, 1, TL)
    dma = pltpu.SemaphoreType.DMA
    vm = pl.BlockSpec(memory_space=pltpu.VMEM)

    def sems(*shape):
        return [dma(shape), dma(shape)]

    outs = pl.pallas_call(
        functools.partial(kernel, nr, nc, block_rows * nr, block_cols * nc),
        out_shape=(
            jax.ShapeDtypeStruct((width, block_rows // nc), F32),
            jax.ShapeDtypeStruct((width, block_cols // nr), F32),
            jax.ShapeDtypeStruct((width, width), F32),
            jax.ShapeDtypeStruct((width, width), F32),
        ),
        in_specs=[pl.BlockSpec(memory_space=pl.ANY)] * 7,
        out_specs=(vm,) * 4,
        scratch_shapes=[
            pltpu.VMEM((1, count), jnp.int32),
            pltpu.VMEM((1, count), jnp.int32),
            pltpu.VMEM((count, TL, TL), F32),
            pltpu.VMEM((width, block_rows), F32),
            pltpu.VMEM((ct, 1, TL), jnp.int32),
            pltpu.VMEM((width, tp * TL), F32),
            pltpu.VMEM((width, width), F32),
            pltpu.VMEM((count, TL), jnp.int32),
            pltpu.SMEM((count, TL), jnp.int32),
            dma((11,)),
            pltpu.VMEM((rt, 2 * width, TL), BF16),
            pltpu.VMEM((ns, nz, QUADS, 2, tps, half, TL), F32),
            pltpu.VMEM((ns * nz, 6, tps, half, TL), F32),
            pltpu.VMEM((ns, nz, 2, tps, half, TL), F32),
            pltpu.VMEM((width, tp * TL), F32),
            pltpu.VMEM((ns, nz, QUADS, 2, tps, half, TL), F32),
            pltpu.VMEM((ct, width, TL), F32),
            pltpu.VMEM((rt, width, TL), F32),
            pltpu.VMEM((nc, rtc, width, TL), F32),
            *[pltpu.VMEM((n, half, 2 * width), F32) for n in (nc, QUADS, nz)] * 2,
            pltpu.VMEM((rtc, width, TL), F32),
            pltpu.VMEM((width, 2 * width), F32),
            *sems(ns * nz, 6),
            *sems(ns, nz),
            *sems(ns, nz),
            *sems(ns * nz, 6),
            *sems(nc),
            *[x for n in (nc, QUADS, nz) for x in sems(n)] * 2,
        ],
        compiler_params=pltpu.CompilerParams(
            collective_id=0, has_side_effects=True, vmem_limit_bytes=56 * 1024 * 1024
        ),
    )(rows, cols, local, u_basis, expo, v_basis, prior)
    return pl.pallas_call(
        hand_out,
        out_shape=tuple(jax.ShapeDtypeStruct(o.shape, o.dtype) for o in outs),
        in_specs=[vm] * 4,
        out_specs=(vm,) * 4,
    )(*outs)


def solution(mesh):
    placed = (
        P("row", "col", None, None, None),
        P("row", "col", None),
        P("row", "col", None),
        P("col"),
        P(None, "row"),
        P(None, ("col", "row")),
        P(),
    )
    return jax.shard_map(
        per_device,
        mesh=mesh,
        in_specs=placed,
        out_specs=(P(None, ("row", "col")), P(None, ("col", "row")), P(), P()),
        check_vma=False,
    )
```
